512 devices in a mesh: vocab: 16 (over y_lo, x, core), dp: 32 (over z, y_hi).
Axes of the slice: x: 4, y: 8 (y_hi: 4, y_lo: 2; y = y_hi * 2 + y_lo), z: 8, core: 2. Of those that a mesh axis runs over, the one named last changes fastest.
Arguments:
- ids: int32 [4096], P('dp'), may hold values from 0 to 65535, as said below
- hidden: bfloat16 [4096, 3584], P('dp', 'vocab'), may hold values from -700 to 700
- table: bfloat16 [3584, 65536], P('dp', 'vocab'), may hold values from -700 to 700
- gain_embed: float32 [3584], P('vocab'), may hold values from 0.1 to 1.9
- gain_hidden: float32 [3584], P('vocab'), may hold values from 0.1 to 1.9
- proj_embed: bfloat16 [3584, 3584], P('vocab', 'dp'), may hold values from -0.125 to 0.125
- proj_hidden: bfloat16 [3584, 3584], P('vocab', 'dp'), may hold values from -0.125 to 0.125
- grad_out: bfloat16 [4096, 3584], P('dp', 'vocab'), may hold values from -6 to 6
Outputs:
- projected: bfloat16 [4096, 3584], P('dp', 'vocab')
- grad_hidden: bfloat16 [4096, 3584], P('dp', 'vocab')
- grad_table: float32 [3584, 65536], P('dp', 'vocab')
- grad_proj_embed: float32 [3584, 3584], P('vocab', 'dp')
- grad_proj_hidden: float32 [3584, 3584], P('vocab', 'dp')
- grad_gains: float32 [2, 3584], P(None, 'vocab')
The draws below stay inside these ranges and needn't reach their ends.
Inputs may be any that keep to these rules, and one draw needn't show every extreme that they name: Within a block of 128 tokens of one index of dp, any number of tokens, up to all of them, may take ids from one vocabulary shard of 4096 entries; in some block all of them do.
All inputs are finite; a program needn't handle non-finite values.
Results may differ from the reference program's by a relative error of at most 0.022.
Values may be sent and summed in bfloat16 or wider, within the bound.
No kernel may reach another device: no remote copies, remote signals or barrier semaphores. Data moves between devices by JAX's collectives and lax.ppermute only.
A program may use at most 64 MiB of HBM per device.

```python
import jax
import jax.numpy as jnp
from jax import lax

D = 3584
VOCAB = 65536
TOK_DEV = 128
TOKENS = 4096
N_VOCAB = 16
N_DP = 32


def rough_scales(key, row_count, col_count):
    row_key, col_key = jax.random.split(key, 2)
    row_scale = jnp.exp(jnp.log(10.0) * jax.random.uniform(row_key, (row_count, 1), jnp.float32))
    trend = jnp.arange(col_count, dtype=jnp.float32)[None, :] / (col_count - 1)
    col_scale = jnp.exp(jnp.log(10.0) * (0.5 * trend + 0.5 * jax.random.uniform(col_key, (1, col_count), jnp.float32)))
    return row_scale * col_scale


def scaled_values(key, row_count, col_count):
    scale_key, value_key = jax.random.split(key, 2)
    scales = rough_scales(scale_key, row_count, col_count)
    values = jnp.clip(jax.random.normal(value_key, (row_count, col_count), jnp.float32), -4.0, 4.0)
    return (values * scales).astype(jnp.bfloat16)


def draw_ids(key, part):
    key = jax.random.fold_in(key, 13)
    shard_key, count_key, forced_key, inner_key, spread_key = jax.random.split(key, 5)
    shard_width = VOCAB // N_VOCAB
    home_shard = jax.random.randint(shard_key, (N_DP, 1), 0, N_VOCAB, dtype=jnp.int32)
    home_count = jax.random.randint(count_key, (N_DP, 1), 0, TOK_DEV + 1, dtype=jnp.int32)
    forced_block = jax.random.randint(forced_key, (), 0, N_DP, dtype=jnp.int32)
    block_numbers = jnp.arange(N_DP, dtype=jnp.int32)[:, None]
    home_count = jnp.where(block_numbers == forced_block, TOK_DEV, home_count)
    positions = jnp.arange(TOK_DEV, dtype=jnp.int32)[None, :]
    inner_ids = home_shard * shard_width + jax.random.randint(inner_key, (N_DP, TOK_DEV), 0, shard_width, dtype=jnp.int32)
    spread_ids = jax.random.randint(spread_key, (N_DP, TOK_DEV), 0, VOCAB, dtype=jnp.int32)
    chosen = jnp.where(positions < home_count, inner_ids, spread_ids)
    return chosen.reshape(TOKENS).astype(jnp.int32)


def draw_hidden(key, part):
    key = jax.random.fold_in(key, 11)
    return scaled_values(key, TOKENS, D)


def draw_table(key, part):
    key = jax.random.fold_in(key, 12)
    return scaled_values(key, VOCAB, D).T


def strengthened(array, own_key, source, target, blocks, factor):
    def block_of(position):
        return (jnp.arange(array.shape[position]) // (array.shape[position] // blocks)).reshape((-1,) + (1,) * (array.ndim - 1 - position))

    first = jax.random.permutation(own_key, blocks)[block_of(target)]
    far = (block_of(target) + blocks // 2) % blocks
    return jnp.where((block_of(source) == first) | (block_of(source) == far), factor * array, array)


def steps_of(stream_key, extent, cuts, least, high):
    level, own = 1.0, jax.random.fold_in(stream_key, 6)
    for dim, shards_of in cuts:
        heights = jnp.exp(jax.random.uniform(jax.random.fold_in(own, dim), (shards_of,), jnp.float32, least / len(cuts), high / len(cuts)))
        level = level * jnp.repeat(heights, extent[dim] // shards_of).reshape([-1 if axis == dim else 1 for axis in range(len(extent))])
    return level


def bell_draw_with(key, extent, scale, limit, shards, heavy, held_as=jnp.bfloat16):
    array = scale * jax.random.normal(key, extent, jnp.float32)
    if shards:
        array = array * steps_of(key, extent, shards, -0.22, 0.18)
    return jnp.clip(strengthened(array, jax.random.fold_in(key, 3), *heavy), -limit, limit).astype(held_as)


def setup_inputs(seed: int = 0) -> dict:
    streams_of = jax.random.split(jax.random.key(seed), 9)
    ids = draw_ids(jax.random.fold_in(streams_of[8], 71), 0)
    hidden = draw_hidden(jax.random.fold_in(streams_of[8], 71), 0)
    table = draw_table(jax.random.fold_in(streams_of[8], 71), 0)
    gain_embed = jnp.clip(1.0 + 0.18 * jax.random.normal(streams_of[3], (D,), jnp.float32), 0.1, 1.9)
    gain_hidden = jnp.clip(1.0 + 0.18 * jax.random.normal(streams_of[4], (D,), jnp.float32), 0.1, 1.9)
    proj_embed = bell_draw_with(streams_of[5], (D, D), (2 * D) ** -0.5, 0.125, ((0, 16), (1, 32)), (0, 1, 32, 2.75))
    proj_hidden = bell_draw_with(streams_of[6], (D, D), (2 * D) ** -0.5, 0.125, ((0, 16), (1, 32)), (0, 1, 32, 2.75))
    grad_out = bell_draw_with(streams_of[7], (TOKENS, D), 1.0, 6.0, ((0, 32), (1, 16)), (0, 1, 32, 2.75))
    return dict(ids=ids, hidden=hidden, table=table, gain_embed=gain_embed, gain_hidden=gain_hidden, proj_embed=proj_embed, proj_hidden=proj_hidden, grad_out=grad_out)


EPS = 1e-06

def inverse_rms(values):
    return lax.rsqrt(lax.optimization_barrier(jnp.sum(values * values, axis=1, keepdims=True)) / D + EPS)

def reference(ids, hidden, table, gain_embed, gain_hidden, proj_embed, proj_hidden, grad_out):
    embedded = jnp.take(table, ids, axis=1).T.astype(jnp.float32)
    hidden_f = hidden.astype(jnp.float32)
    inv_embed = inverse_rms(embedded)
    inv_hidden = inverse_rms(hidden_f)
    norm_embed = embedded * inv_embed
    norm_hidden = hidden_f * inv_hidden
    left = (norm_embed * gain_embed).astype(jnp.bfloat16)
    right = (norm_hidden * gain_hidden).astype(jnp.bfloat16)
    feat_width = D // N_VOCAB

    def feature_block(running, block_index):
        first_col = block_index * feat_width
        left_block = lax.dynamic_slice_in_dim(left, first_col, feat_width, 1)
        right_block = lax.dynamic_slice_in_dim(right, first_col, feat_width, 1)
        embed_rows = lax.dynamic_slice_in_dim(proj_embed, first_col, feat_width, 0)
        hidden_rows = lax.dynamic_slice_in_dim(proj_hidden, first_col, feat_width, 0)
        partial_sum = jnp.dot(left_block, embed_rows, preferred_element_type=jnp.float32) + jnp.dot(right_block, hidden_rows, preferred_element_type=jnp.float32)
        rounded = lax.optimization_barrier(partial_sum.astype(jnp.bfloat16))
        return (running + rounded.astype(jnp.float32), None)
    summed, _ = lax.scan(feature_block, jnp.zeros((TOKENS, D), jnp.float32), jnp.arange(N_VOCAB, dtype=jnp.int32))
    projected = summed.astype(jnp.bfloat16)
    grad_left = jnp.dot(grad_out, proj_embed.T, preferred_element_type=jnp.float32)
    grad_right = jnp.dot(grad_out, proj_hidden.T, preferred_element_type=jnp.float32)

    def token_block(running, block_index):
        first_row = block_index * TOK_DEV
        left_block = lax.dynamic_slice_in_dim(left, first_row, TOK_DEV, 0)
        right_block = lax.dynamic_slice_in_dim(right, first_row, TOK_DEV, 0)
        grad_block = lax.dynamic_slice_in_dim(grad_out, first_row, TOK_DEV, 0)
        embed_term = lax.optimization_barrier(jnp.dot(left_block.T, grad_block, preferred_element_type=jnp.float32).astype(jnp.bfloat16))
        hidden_term = lax.optimization_barrier(jnp.dot(right_block.T, grad_block, preferred_element_type=jnp.float32).astype(jnp.bfloat16))
        return ((running[0] + embed_term.astype(jnp.float32), running[1] + hidden_term.astype(jnp.float32)), None)
    zeros_square = jnp.zeros((D, D), jnp.float32)
    weight_grads, _ = lax.scan(token_block, (zeros_square, zeros_square), jnp.arange(N_DP, dtype=jnp.int32))
    grad_gains = jnp.stack([lax.optimization_barrier(jnp.sum(grad_left * norm_embed, axis=0)), lax.optimization_barrier(jnp.sum(grad_right * norm_hidden, axis=0))])
    dn_embed = grad_left * gain_embed
    dn_hidden = grad_right * gain_hidden
    coef_embed = lax.optimization_barrier(jnp.sum(dn_embed * norm_embed, axis=1, keepdims=True)) / D
    coef_hidden = lax.optimization_barrier(jnp.sum(dn_hidden * norm_hidden, axis=1, keepdims=True)) / D
    grad_embedded = (inv_embed * (dn_embed - norm_embed * coef_embed)).astype(jnp.bfloat16)
    grad_hidden = (inv_hidden * (dn_hidden - norm_hidden * coef_hidden)).astype(jnp.bfloat16)
    grad_table = jnp.zeros((D, VOCAB), jnp.float32).at[:, ids].add(grad_embedded.astype(jnp.float32).T)
    return (projected, grad_hidden, grad_table, weight_grads[0], weight_grads[1], grad_gains)
```

```python
import jax
import jax.numpy as jnp
from jax import lax
from jax.experimental import pallas as pl
from jax.sharding import Mesh
from jax.sharding import PartitionSpec as P

EPS = 1e-06
GROUPS = 8
BF16 = jnp.bfloat16
F32 = jnp.float32
DP = ("z", "yhi")
ALL = ("vocab", "z", "yhi")


def gather(x, axes, count):
    return lax.all_to_all(
        jnp.broadcast_to(x[None], (count,) + x.shape), axes, 0, 0, tiled=True
    )


def one_hot_of(ids, width):
    rows = lax.broadcasted_iota(jnp.int32, (width, ids.shape[1]), 0)
    return jnp.where(rows == ids % width, 1.0, 0.0).astype(BF16)


def lookup_kernel(ids_ref, table_ref, out_ref):
    ids = ids_ref[0]
    width = table_ref.shape[1] // GROUPS
    one_hot = one_hot_of(ids, width)
    group = lax.div(jnp.where(ids < 0, -width, ids), width)
    total = jnp.zeros(out_ref.shape[1:], F32)
    for k in range(GROUPS):
        picked = jnp.dot(
            table_ref[:, k * width : (k + 1) * width], one_hot, preferred_element_type=F32
        )
        total = jnp.where(group == k, picked, total)
    out_ref[0] = total.astype(BF16)


def lookup(ids, table):
    blocks, _, rows = ids.shape
    cols, entries = table.shape
    return pl.pallas_call(
        lookup_kernel,
        grid=(blocks,),
        in_specs=[
            pl.BlockSpec((1, 1, rows), lambda i: (i, 0, 0)),
            pl.BlockSpec((cols, entries), lambda i: (0, 0)),
        ],
        out_specs=pl.BlockSpec((1, cols, rows), lambda i: (i, 0, 0)),
        out_shape=jax.ShapeDtypeStruct((blocks, cols, rows), BF16),
        cost_estimate=pl.CostEstimate(
            flops=2 * blocks * rows * cols * entries,
            bytes_accessed=2 * cols * (entries + blocks * rows),
            transcendentals=0,
        ),
    )(ids, table)


def scatter_kernel(ids_ref, rows_ref, out_ref):
    ids = ids_ref[0]
    width = out_ref.shape[1] // GROUPS
    one_hot = one_hot_of(ids, width)
    group = lax.div(jnp.where(ids < 0, -width, ids), width)
    values = rows_ref[0]

    @pl.when(pl.program_id(0) == 0)
    def _():
        out_ref[...] = jnp.zeros_like(out_ref)

    for k in range(GROUPS):
        inside = jnp.where(group == k, 1.0, 0.0).astype(BF16)
        out_ref[:, k * width : (k + 1) * width] += lax.dot_general(
            values * inside, one_hot, (((1,), (1,)), ((), ())), preferred_element_type=F32
        )


def scatter(ids, values, entries):
    blocks, cols, rows = values.shape
    return pl.pallas_call(
        scatter_kernel,
        grid=(blocks,),
        in_specs=[
            pl.BlockSpec((1, 1, rows), lambda i: (i, 0, 0)),
            pl.BlockSpec((1, cols, rows), lambda i: (i, 0, 0)),
        ],
        out_specs=pl.BlockSpec((cols, entries), lambda i: (0, 0)),
        out_shape=jax.ShapeDtypeStruct((cols, entries), F32),
        cost_estimate=pl.CostEstimate(
            flops=2 * blocks * rows * cols * entries,
            bytes_accessed=cols * (4 * entries + 2 * blocks * rows),
            transcendentals=0,
        ),
    )(ids, values)


def per_device(ids, hidden, table, gain_embed, gain_hidden, proj_embed, proj_hidden, grad_out):
    v = lax.axis_index("vocab")
    nv = lax.axis_size("vocab")
    na, nb = lax.axis_size("z"), lax.axis_size("yhi")
    nd = na * nb
    d = lax.axis_index("z") * nb + lax.axis_index("yhi")
    odd = d % 2 == 1
    toks, fw = hidden.shape
    cw, entries = table.shape
    full = fw * nv

    def swap_route(c):
        return [
            (i * nd + j, (j // 2) * nd + 2 * i + (j % 2 + c) % 2)
            for i in range(nv)
            for j in range(nd)
        ]

    def swap_back(c):
        return [(b, a) for a, b in swap_route(c)]

    turn = [
        (i * nd + a * nb + b, (2 * a + i % 2) * nd + (i // 2) * nb + b)
        for i in range(nv)
        for a in range(na)
        for b in range(nb)
    ]
    turn_back = [(b, a) for a, b in turn]

    all_ids = gather(ids, DP, nd)
    local_ids = (all_ids - v * entries).reshape(nv, 1, 2 * toks)
    weights = jnp.concatenate([proj_embed, proj_hidden], axis=0).T
    weights = gather(weights, "yhi", nb).reshape(nb * cw, 2 * fw)
    cot = gather(lax.ppermute(grad_out.T, ALL, turn), "vocab", nv)
    cot = cot.reshape(na, 2 * fw, toks)

    pieces = lax.all_to_all(lookup(local_ids, table), "vocab", 0, 0, tiled=True)
    cols = jnp.sum(pieces.astype(F32), axis=0).astype(BF16)
    first, second = cols[:, :toks], cols[:, toks:]
    got0 = lax.ppermute(jnp.where(odd, second, first), ALL, swap_route(0))
    got1 = lax.ppermute(jnp.where(odd, first, second), ALL, swap_route(1))
    embed = jnp.concatenate(
        [jnp.where(odd, got1, got0), jnp.where(odd, got0, got1)], axis=0
    ).astype(F32)

    hid = hidden.T.astype(F32)
    gain_e, gain_h = gain_embed[:, None], gain_hidden[:, None]
    hid_total = jnp.sum(gather(jnp.sum(hid * hid, axis=0), "vocab", nv), axis=0)
    inv_hidden = lax.rsqrt(hid_total / full + EPS)[None]
    norm_hidden = hid * inv_hidden
    right = gather((norm_hidden * gain_h).astype(BF16), "z", na)

    shares = jnp.stack(
        [
            lax.dot_general(
                weights, cot[a], (((0,), (0,)), ((), ())), preferred_element_type=F32
            ).astype(BF16)
            for a in range(na)
        ]
    )
    grads = jnp.sum(lax.all_to_all(shares, "z", 0, 0, tiled=True).astype(F32), axis=0)
    grad_left, grad_right = grads[:fw], grads[fw:]
    dn_embed, dn_hidden = grad_left * gain_e, grad_right * gain_h

    stats = jnp.stack(
        [
            jnp.sum(embed * embed, axis=0),
            jnp.sum(dn_embed * embed, axis=0),
            jnp.sum(dn_hidden * norm_hidden, axis=0),
        ]
    )
    stats = jnp.sum(gather(stats, "vocab", nv), axis=0)
    inv_embed = lax.rsqrt(stats[0] / full + EPS)[None]
    norm_embed = embed * inv_embed
    coef_embed = stats[1][None] * inv_embed / full
    coef_hidden = stats[2][None] / full
    grad_embedded = (inv_embed * (dn_embed - norm_embed * coef_embed)).astype(BF16)
    grad_hidden = (inv_hidden * (dn_hidden - norm_hidden * coef_hidden)).astype(BF16)

    low, high = grad_embedded[:cw], grad_embedded[cw:]
    got0 = lax.ppermute(jnp.where(odd, high, low), ALL, swap_back(0))
    got1 = lax.ppermute(jnp.where(odd, low, high), ALL, swap_back(1))
    mine = jnp.concatenate(
        [jnp.where(odd, got1, got0), jnp.where(odd, got0, got1)], axis=1
    )
    grad_table = scatter(local_ids, gather(mine, "vocab", nv), entries)

    left = gather((norm_embed * gain_e).astype(BF16), "z", na)
    both = jnp.concatenate([left, right], axis=1)
    terms = jnp.stack(
        [jnp.dot(weights, both[a], preferred_element_type=F32).astype(BF16) for a in range(na)]
    ).reshape(nv, fw, toks)
    terms = lax.all_to_all(terms, "vocab", 0, 0, tiled=True)
    projected = jnp.sum(terms.astype(F32), axis=0).astype(BF16)
    projected = lax.ppermute(projected, ALL, turn_back).T
    weight_terms = lax.dot_general(
        cot, both, (((0, 2), (0, 2)), ((), ())), preferred_element_type=F32
    ).astype(BF16)
    weight_terms = lax.all_to_all(weight_terms.reshape(nb, cw, 2 * fw), "yhi", 0, 0, tiled=True)
    weight_grads = jnp.sum(weight_terms.astype(F32), axis=0).T

    gains = jnp.concatenate(
        [jnp.sum(grad_left * norm_embed, axis=1), jnp.sum(grad_right * norm_hidden, axis=1)]
    )
    grad_gains = jnp.sum(gather(gains, DP, nd), axis=0).reshape(2, fw)
    return (projected, grad_hidden.T, grad_table, weight_grads[:fw], weight_grads[fw:], grad_gains)


def solution(mesh):
    nv, nd = mesh.shape["vocab"], mesh.shape["dp"]
    nb = min(4, nd)
    split = Mesh(mesh.devices.reshape(nv, nd // nb, nb), ALL)
    rows = P(DP, "vocab")
    return jax.shard_map(
        per_device,
        mesh=split,
        in_specs=(
            P(DP),
            rows,
            rows,
            P("vocab"),
            P("vocab"),
            P("vocab", DP),
            P("vocab", DP),
            rows,
        ),
        out_specs=(rows, rows, rows, P("vocab", DP), P("vocab", DP), P(None, "vocab")),
        check_vma=False,
    )
```

```python
import jax
import jax.numpy as jnp
from jax import lax
from jax.experimental import pallas as pl
from jax.experimental.pallas import tpu as pltpu
from jax.sharding import Mesh
from jax.sharding import PartitionSpec as P

EPS = 1e-06
GROUPS = 8
BF16 = jnp.bfloat16
F32 = jnp.float32
DP = ("z", "yhi")
ALL = ("vocab", "z", "yhi")


def gather(x, axes, count):
    return lax.all_to_all(
        jnp.broadcast_to(x[None], (count,) + x.shape), axes, 0, 0, tiled=True
    )


def one_hot_of(ids, width):
    rows = lax.broadcasted_iota(jnp.int32, (width, ids.shape[1]), 0)
    return jnp.where(rows == ids % width, 1.0, 0.0).astype(BF16)


def group_of(ids, width):
    return lax.div(jnp.where(ids < 0, -width, ids), width)


def lookup_kernel(ids_ref, table_ref, out_ref):
    ids = ids_ref[0]
    width = table_ref.shape[1]
    cols = table_ref.shape[0] // GROUPS
    picked = jnp.dot(
        table_ref[...], one_hot_of(ids, width), preferred_element_type=F32
    )
    group = group_of(ids, width)
    total = jnp.zeros((cols, ids.shape[1]), F32)
    for k in range(GROUPS):
        total = jnp.where(group == k, picked[k * cols : (k + 1) * cols], total)
    out_ref[0] = total.astype(BF16)


def lookup(ids, table):
    blocks, _, rows = ids.shape
    cols, entries = table.shape
    width = entries // GROUPS
    stacked = table.reshape(cols, GROUPS, width).transpose(1, 0, 2).reshape(cols * GROUPS, width)
    return pl.pallas_call(
        lookup_kernel,
        grid=(blocks,),
        in_specs=[
            pl.BlockSpec((1, 1, rows), lambda i: (i, 0, 0)),
            pl.BlockSpec((cols * GROUPS, width), lambda i: (0, 0)),
        ],
        out_specs=pl.BlockSpec((1, cols, rows), lambda i: (i, 0, 0)),
        out_shape=jax.ShapeDtypeStruct((blocks, cols, rows), BF16),
        cost_estimate=pl.CostEstimate(
            flops=2 * blocks * rows * cols * entries,
            bytes_accessed=2 * cols * (entries + blocks * rows),
            transcendentals=0,
        ),
    )(ids, stacked)


def scatter_kernel(ids_ref, rows_ref, out_ref):
    width = out_ref.shape[1] // GROUPS
    cols = out_ref.shape[0]
    parts = ids_ref.shape[0]
    ids = jnp.concatenate([ids_ref[i] for i in range(parts)], axis=1)
    values = jnp.concatenate([rows_ref[i] for i in range(parts)], axis=1)
    group = group_of(ids, width)
    spread = jnp.concatenate(
        [values * jnp.where(group == k, 1.0, 0.0).astype(BF16) for k in range(GROUPS)], axis=0
    )
    sums = lax.dot_general(
        spread, one_hot_of(ids, width), (((1,), (1,)), ((), ())), preferred_element_type=F32
    )

    @pl.when(pl.program_id(0) == 0)
    def _():
        for k in range(GROUPS):
            out_ref[:, k * width : (k + 1) * width] = sums[k * cols : (k + 1) * cols]

    @pl.when(pl.program_id(0) > 0)
    def _():
        for k in range(GROUPS):
            out_ref[:, k * width : (k + 1) * width] += sums[k * cols : (k + 1) * cols]


def scatter(ids, values, entries):
    blocks, cols, rows = values.shape
    parts = 4
    return pl.pallas_call(
        scatter_kernel,
        grid=(blocks // parts,),
        in_specs=[
            pl.BlockSpec((parts, 1, rows), lambda i: (i, 0, 0)),
            pl.BlockSpec((parts, cols, rows), lambda i: (i, 0, 0)),
        ],
        out_specs=pl.BlockSpec((cols, entries), lambda i: (0, 0)),
        out_shape=jax.ShapeDtypeStruct((cols, entries), F32),
        cost_estimate=pl.CostEstimate(
            flops=2 * blocks * rows * cols * entries,
            bytes_accessed=cols * (4 * entries + 2 * blocks * rows),
            transcendentals=0,
        ),
        compiler_params=pltpu.CompilerParams(vmem_limit_bytes=32 * 1024 * 1024),
    )(ids, values)


def grad_kernel(weights_ref, cot_ref, out_ref):
    weights = weights_ref[...].T
    for a in range(cot_ref.shape[0]):
        out_ref[a] = jnp.dot(weights, cot_ref[a], preferred_element_type=F32).astype(BF16)


def grad_products(weights, cot):
    na, outs, toks = cot.shape
    feats = weights.shape[1]
    return pl.pallas_call(
        grad_kernel,
        out_shape=jax.ShapeDtypeStruct((na, feats, toks), BF16),
        cost_estimate=pl.CostEstimate(
            flops=2 * na * outs * feats * toks,
            bytes_accessed=2 * (outs * feats + na * (outs + feats) * toks),
            transcendentals=0,
        ),
        compiler_params=pltpu.CompilerParams(vmem_limit_bytes=16 * 1024 * 1024),
    )(weights, cot)


def out_kernel(weights_ref, cot_ref, normed_ref, out_ref, sums_ref):
    weights = weights_ref[...]
    feats = weights.shape[1]
    for a in range(cot_ref.shape[0]):
        out_ref[a] = jnp.dot(
            weights, normed_ref[a, :feats], preferred_element_type=F32
        ).astype(BF16)
    cot = jnp.concatenate([cot_ref[a] for a in range(cot_ref.shape[0])], axis=1)
    normed = jnp.concatenate([normed_ref[a, :feats] for a in range(cot_ref.shape[0])], axis=1)
    sums_ref[...] = lax.dot_general(
        cot, normed, (((1,), (1,)), ((), ())), preferred_element_type=F32
    ).astype(BF16)


def out_products(weights, cot, normed):
    na, outs, toks = cot.shape
    feats = weights.shape[1]
    return pl.pallas_call(
        out_kernel,
        out_shape=(
            jax.ShapeDtypeStruct((na, outs, toks), BF16),
            jax.ShapeDtypeStruct((outs, feats), BF16),
        ),
        cost_estimate=pl.CostEstimate(
            flops=4 * na * outs * feats * toks,
            bytes_accessed=2 * (2 * outs * feats + na * (2 * outs + feats) * toks),
            transcendentals=0,
        ),
        compiler_params=pltpu.CompilerParams(vmem_limit_bytes=16 * 1024 * 1024),
    )(weights, cot, normed)


def per_device(ids, hidden, table, gain_embed, gain_hidden, proj_embed, proj_hidden, grad_out):
    v = lax.axis_index("vocab")
    nv = lax.axis_size("vocab")
    na, nb = lax.axis_size("z"), lax.axis_size("yhi")
    nd = na * nb
    d = lax.axis_index("z") * nb + lax.axis_index("yhi")
    odd = d % 2 == 1
    toks, fw = hidden.shape
    cw, entries = table.shape
    full = fw * nv

    def swap_route(c):
        return [
            (i * nd + j, (j // 2) * nd + 2 * i + (j % 2 + c) % 2)
            for i in range(nv)
            for j in range(nd)
        ]

    def swap_back(c):
        return [(b, a) for a, b in swap_route(c)]

    def in_order(got0, got1, axis):
        return jnp.concatenate(
            [jnp.where(odd, got1, got0), jnp.where(odd, got0, got1)], axis=axis
        )

    turn = [
        (i * nd + a * nb + b, (2 * a + i % 2) * nd + (i // 2) * nb + b)
        for i in range(nv)
        for a in range(na)
        for b in range(nb)
    ]
    turn_back = [(b, a) for a, b in turn]

    weights = jnp.concatenate([proj_embed, proj_hidden], axis=0).T
    weights = gather(weights, "yhi", nb).reshape(nb * cw, 2 * fw)

    digits = jnp.stack([ids // 256, ids % 256]).astype(BF16)
    digits = in_order(
        lax.ppermute(digits, ALL, swap_route(0)), lax.ppermute(digits, ALL, swap_route(1)), 0
    )
    cot = lax.ppermute(grad_out.T, ALL, turn)
    cot = jnp.concatenate([cot, jnp.pad(digits, ((0, 12), (0, 0)))], axis=0)
    cot = gather(cot, "vocab", nv)
    digits = cot[:, fw : fw + 4].astype(jnp.int32)
    cot = cot[:, :fw].reshape(na, 2 * fw, toks)
    all_ids = 256 * digits[:, 0::2] + digits[:, 1::2]
    local_ids = (all_ids - v * entries).reshape(nv, 1, 2 * toks)

    grads = lax.psum_scatter(
        grad_products(weights, cot).reshape(na * 2 * fw, toks), "z", scatter_dimension=0, tiled=True
    ).astype(F32)

    pieces = lax.all_to_all(lookup(local_ids, table), "vocab", 0, 0, tiled=True)
    cols = jnp.sum(pieces.astype(F32), axis=0).astype(BF16)
    first, second = cols[:, :toks], cols[:, toks:]
    embed = in_order(
        lax.ppermute(jnp.where(odd, second, first), ALL, swap_route(0)),
        lax.ppermute(jnp.where(odd, first, second), ALL, swap_route(1)),
        0,
    ).astype(F32)

    hid = hidden.T.astype(F32)
    gain_e, gain_h = gain_embed[:, None], gain_hidden[:, None]
    grad_left, grad_right = grads[:fw], grads[fw:]
    dn_embed, dn_hidden = grad_left * gain_e, grad_right * gain_h
    stats = jnp.stack(
        [
            jnp.sum(embed * embed, axis=0),
            jnp.sum(hid * hid, axis=0),
            jnp.sum(dn_embed * embed, axis=0),
            jnp.sum(dn_hidden * hid, axis=0),
        ]
    )
    stats = jnp.sum(gather(stats, "vocab", nv), axis=0)
    inv_embed = lax.rsqrt(stats[0] / full + EPS)[None]
    inv_hidden = lax.rsqrt(stats[1] / full + EPS)[None]
    norm_embed, norm_hidden = embed * inv_embed, hid * inv_hidden
    coef_embed = stats[2][None] * inv_embed / full
    coef_hidden = stats[3][None] * inv_hidden / full
    grad_embedded = (inv_embed * (dn_embed - norm_embed * coef_embed)).astype(BF16)
    grad_hidden = (inv_hidden * (dn_hidden - norm_hidden * coef_hidden)).astype(BF16)

    gains = jnp.concatenate(
        [jnp.sum(grad_left * norm_embed, axis=1), jnp.sum(grad_right * norm_hidden, axis=1)]
    )
    gains_high = gains.astype(BF16)
    gains_low = (gains - gains_high.astype(F32)).astype(BF16)
    lines = 2 * fw // toks + 1
    extra = jnp.pad(
        jnp.stack([gains_high, gains_low]), ((0, 0), (0, lines * toks - 2 * fw))
    ).reshape(2 * lines, toks)
    extra = jnp.pad(extra, ((0, -2 * lines % 16), (0, 0)))
    normed = gather(
        jnp.concatenate(
            [(norm_embed * gain_e).astype(BF16), (norm_hidden * gain_h).astype(BF16), extra], axis=0
        ),
        "z",
        na,
    )
    gains = jnp.sum(
        normed[:, 2 * fw : 2 * fw + 2 * lines].reshape(na, 2, lines * toks).astype(F32), axis=(0, 1)
    )[: 2 * fw]

    low, high = grad_embedded[:cw], grad_embedded[cw:]
    mine = in_order(
        lax.ppermute(jnp.where(odd, high, low), ALL, swap_back(0)),
        lax.ppermute(jnp.where(odd, low, high), ALL, swap_back(1)),
        1,
    )
    grad_table = scatter(local_ids, gather(mine, "vocab", nv), entries)

    terms, weight_terms = out_products(weights, cot, normed)
    terms = lax.all_to_all(terms.reshape(nv, fw, toks), "vocab", 0, 0, tiled=True)
    projected = jnp.sum(terms.astype(F32), axis=0).astype(BF16)
    projected = lax.ppermute(projected, ALL, turn_back).T
    gains = jnp.pad(gains.astype(BF16)[None], ((0, 15), (0, 0)))
    weight_terms = jnp.concatenate(
        [
            weight_terms.reshape(nb, cw, 2 * fw),
            jnp.broadcast_to(gains[None], (nb,) + gains.shape),
        ],
        axis=1,
    )
    weight_terms = lax.psum_scatter(
        weight_terms.reshape(nb * (cw + 16), 2 * fw), "yhi", scatter_dimension=0, tiled=True
    ).astype(F32)
    weight_grads = weight_terms[:cw].T
    grad_gains = weight_terms[cw].reshape(2, fw)
    return (projected, grad_hidden.T, grad_table, weight_grads[:fw], weight_grads[fw:], grad_gains)


def solution(mesh):
    nv, nd = mesh.shape["vocab"], mesh.shape["dp"]
    nb = min(4, nd)
    split = Mesh(mesh.devices.reshape(nv, nd // nb, nb), ALL)
    rows = P(DP, "vocab")
    return jax.shard_map(
        per_device,
        mesh=split,
        in_specs=(
            P(DP),
            rows,
            rows,
            P("vocab"),
            P("vocab"),
            P("vocab", DP),
            P("vocab", DP),
            rows,
        ),
        out_specs=(rows, rows, rows, P("vocab", DP), P("vocab", DP), P(None, "vocab")),
        check_vma=False,
    )
```

```python
import functools

import jax
import jax.numpy as jnp
from jax import lax
from jax.experimental import pallas as pl
from jax.experimental.pallas import tpu as pltpu
from jax.sharding import Mesh
from jax.sharding import PartitionSpec as P

EPS = 1e-06
GROUPS = 8
BF16 = jnp.bfloat16
F32 = jnp.float32
DP = ("z", "yhi")
ALL = ("vocab", "z", "yhi")


def gather(x, axes, count):
    return lax.all_to_all(
        jnp.broadcast_to(x[None], (count,) + x.shape), axes, 0, 0, tiled=True
    )


def one_hot_of(ids, width):
    rows = lax.broadcasted_iota(jnp.int32, (width, ids.shape[1]), 0)
    return jnp.where(rows == ids % width, 1.0, 0.0).astype(BF16)


def group_of(ids, width):
    return lax.div(jnp.where(ids < 0, -width, ids), width)


def lookup_kernel(ids_ref, table_ref, out_ref):
    parts, _, rows = ids_ref.shape
    width = table_ref.shape[1]
    cols = table_ref.shape[0] // GROUPS
    ids = jnp.concatenate([ids_ref[i] for i in range(parts)], axis=1)
    picked = jnp.dot(
        table_ref[...], one_hot_of(ids, width), preferred_element_type=F32
    )
    group = group_of(ids, width)
    total = jnp.zeros((cols, ids.shape[1]), F32)
    for k in range(GROUPS):
        total = jnp.where(group == k, picked[k * cols : (k + 1) * cols], total)
    for i in range(parts):
        out_ref[i] = total[:, i * rows : (i + 1) * rows].astype(BF16)


def lookup(ids, table):
    blocks, _, rows = ids.shape
    cols, entries = table.shape
    width = entries // GROUPS
    parts = 4
    stacked = table.reshape(cols, GROUPS, width).transpose(1, 0, 2).reshape(cols * GROUPS, width)
    return pl.pallas_call(
        lookup_kernel,
        grid=(blocks // parts,),
        in_specs=[
            pl.BlockSpec((parts, 1, rows), lambda i: (i, 0, 0)),
            pl.BlockSpec((cols * GROUPS, width), lambda i: (0, 0)),
        ],
        out_specs=pl.BlockSpec((parts, cols, rows), lambda i: (i, 0, 0)),
        out_shape=jax.ShapeDtypeStruct((blocks, cols, rows), BF16),
        cost_estimate=pl.CostEstimate(
            flops=2 * blocks * rows * cols * entries,
            bytes_accessed=2 * cols * (entries + blocks * rows),
            transcendentals=0,
        ),
        compiler_params=pltpu.CompilerParams(vmem_limit_bytes=32 * 1024 * 1024),
    )(ids, stacked)


def scatter_kernel(ids_ref, rows_ref, out_ref):
    width = out_ref.shape[1] // GROUPS
    cols = out_ref.shape[0]
    parts = ids_ref.shape[0]
    ids = jnp.concatenate([ids_ref[i] for i in range(parts)], axis=1)
    values = jnp.concatenate(
        [rows_ref[i, j * cols : (j + 1) * cols] for i in range(parts) for j in range(2)], axis=1
    )
    group = group_of(ids, width)
    spread = jnp.concatenate(
        [values * jnp.where(group == k, 1.0, 0.0).astype(BF16) for k in range(GROUPS)], axis=0
    )
    sums = lax.dot_general(
        spread, one_hot_of(ids, width), (((1,), (1,)), ((), ())), preferred_element_type=F32
    )

    @pl.when(pl.program_id(0) == 0)
    def _():
        for k in range(GROUPS):
            out_ref[:, k * width : (k + 1) * width] = sums[k * cols : (k + 1) * cols]

    @pl.when(pl.program_id(0) > 0)
    def _():
        for k in range(GROUPS):
            out_ref[:, k * width : (k + 1) * width] += sums[k * cols : (k + 1) * cols]


def scatter(ids, values, entries):
    blocks, rows, toks = values.shape
    cols = rows // 4
    parts = 4
    return pl.pallas_call(
        scatter_kernel,
        grid=(blocks // parts,),
        in_specs=[
            pl.BlockSpec((parts, 1, 2 * toks), lambda i: (i, 0, 0)),
            pl.BlockSpec((parts, 2 * cols, toks), lambda i: (i, 1, 0)),
        ],
        out_specs=pl.BlockSpec((cols, entries), lambda i: (0, 0)),
        out_shape=jax.ShapeDtypeStruct((cols, entries), F32),
        cost_estimate=pl.CostEstimate(
            flops=4 * blocks * toks * cols * entries,
            bytes_accessed=cols * (4 * entries + 4 * blocks * toks),
            transcendentals=0,
        ),
        compiler_params=pltpu.CompilerParams(vmem_limit_bytes=32 * 1024 * 1024),
    )(ids, values)


def cot_columns(cot_ref, b, cw):
    half = b % 2 * cw
    return jnp.concatenate(
        [cot_ref[i, half : half + cw] for i in range(b // 2, cot_ref.shape[0], 2)], axis=0
    )


def grad_kernel(cw, weights_ref, cot_ref, out_ref):
    nb, feats, _ = out_ref.shape
    weights = jnp.concatenate(
        [weights_ref[a, :cw, :feats] for a in range(weights_ref.shape[0])], axis=0
    ).T
    for b in range(nb):
        out_ref[b] = jnp.dot(
            weights, cot_columns(cot_ref, b, cw), preferred_element_type=F32
        ).astype(BF16)


def grad_products(weights, cot, nb, cw, feats):
    na, toks = weights.shape[0], cot.shape[2]
    return pl.pallas_call(
        functools.partial(grad_kernel, cw),
        out_shape=jax.ShapeDtypeStruct((nb, feats, toks), BF16),
        cost_estimate=pl.CostEstimate(
            flops=2 * na * cw * feats * nb * toks,
            bytes_accessed=2 * (weights.size + cot.size + nb * feats * toks),
            transcendentals=0,
        ),
        compiler_params=pltpu.CompilerParams(vmem_limit_bytes=16 * 1024 * 1024),
    )(weights, cot)


def out_kernel(cw, feats, weights_ref, cot_ref, normed_ref, mine_ref, out_ref, sums_ref):
    na, nb = weights_ref.shape[0], normed_ref.shape[0]
    toks = normed_ref.shape[2]
    weights = jnp.concatenate([weights_ref[a, :cw, :feats] for a in range(na)], axis=0)
    for b in range(nb):
        terms = jnp.dot(weights, normed_ref[b, :feats], preferred_element_type=F32).astype(BF16)
        for a in range(na):
            half = b % 2 * cw
            out_ref[2 * a + b // 2, half : half + cw] = terms[a * cw : (a + 1) * cw]
    mine = mine_ref[...]
    for i in range(out_ref.shape[0]):
        out_ref[i, 2 * cw :] = mine
    cot = jnp.concatenate([cot_columns(cot_ref, b, cw) for b in range(nb)], axis=1)
    normed = jnp.concatenate([normed_ref[b, :feats] for b in range(nb)], axis=1)
    sums = lax.dot_general(
        cot, normed, (((1,), (1,)), ((), ())), preferred_element_type=F32
    ).astype(BF16)
    gains = jnp.zeros((16, toks), F32)
    for b in range(nb):
        gains += normed_ref[b, feats : feats + 16].astype(F32)
        gains += normed_ref[b, feats + 16 : feats + 32].astype(F32)
    for a in range(na):
        sums_ref[a, :cw] = sums[a * cw : (a + 1) * cw]
        sums_ref[a, cw:] = jnp.zeros((16, feats), BF16)
        sums_ref[a, cw:, :toks] = gains.astype(BF16)


def out_products(weights, cot, normed, mine, cw, feats):
    na, (nb, _, toks) = weights.shape[0], normed.shape
    return pl.pallas_call(
        functools.partial(out_kernel, cw, feats),
        out_shape=(
            jax.ShapeDtypeStruct((2 * na, 4 * cw, toks), BF16),
            jax.ShapeDtypeStruct((na, cw + 16, feats), BF16),
        ),
        cost_estimate=pl.CostEstimate(
            flops=4 * na * cw * feats * nb * toks,
            bytes_accessed=2 * (weights.size + 2 * cot.size + normed.size + na * cw * feats),
            transcendentals=0,
        ),
        compiler_params=pltpu.CompilerParams(vmem_limit_bytes=32 * 1024 * 1024),
    )(weights, cot, normed, mine)


def finish_kernel(cw, fw, lines, sums_ref, done_ref, embed_ref, hidden_ref, gains_ref):
    toks = done_ref.shape[1]
    sums = sums_ref[...].astype(F32)
    turned = sums.T
    embed_ref[...] = turned[:fw, :cw]
    hidden_ref[...] = turned[fw:, :cw]
    gains = jnp.concatenate(
        [sums[cw + i : cw + i + 1, :toks] for i in range(lines)], axis=1
    )
    gains_ref[0:1, :] = gains[:, :fw]
    gains_ref[1:2, :] = gains[:, fw : 2 * fw]


def finish(sums, done, cw, fw, lines):
    return pl.pallas_call(
        functools.partial(finish_kernel, cw, fw, lines),
        out_shape=(
            jax.ShapeDtypeStruct((fw, cw), F32),
            jax.ShapeDtypeStruct((fw, cw), F32),
            jax.ShapeDtypeStruct((2, fw), F32),
        ),
        cost_estimate=pl.CostEstimate(
            flops=0, bytes_accessed=2 * sums.size + 8 * fw * cw, transcendentals=0
        ),
    )(sums, done)


def per_device(ids, hidden, table, gain_embed, gain_hidden, proj_embed, proj_hidden, grad_out):
    v = lax.axis_index("vocab")
    nv = lax.axis_size("vocab")
    na, nb = lax.axis_size("z"), lax.axis_size("yhi")
    nd = na * nb
    d = lax.axis_index("z") * nb + lax.axis_index("yhi")
    odd = d % 2 == 1
    toks, fw = hidden.shape
    cw, entries = table.shape
    full = fw * nv

    def swap_route(c):
        return [
            (i * nd + j, (j // 2) * nd + 2 * i + (j % 2 + c) % 2)
            for i in range(nv)
            for j in range(nd)
        ]

    def swap_back(c):
        return [(b, a) for a, b in swap_route(c)]

    def in_order(got0, got1, axis):
        return jnp.concatenate(
            [jnp.where(odd, got1, got0), jnp.where(odd, got0, got1)], axis=axis
        )

    def turn(c):
        return [
            (
                (2 * a2 + b1) * nd + a * nb + 2 * core + x,
                (2 * a2 + core) * nd + a * nb + 2 * b1 + (x + c) % 2,
            )
            for a2 in range(na)
            for b1 in range(2)
            for a in range(na)
            for core in range(2)
            for x in range(2)
        ]

    def turn_back(c):
        return [(b, a) for a, b in turn(c)]

    weights = jnp.concatenate([proj_embed, proj_hidden], axis=0).T
    weights = jnp.pad(weights, ((0, -cw % 128), (0, -2 * fw % 512)))
    weights = lax.all_gather(weights, "z")

    digits = jnp.stack([ids // 256, ids % 256]).astype(BF16)
    digits = in_order(
        lax.ppermute(digits, ALL, swap_route(0)), lax.ppermute(digits, ALL, swap_route(1)), 0
    )
    first, second = grad_out.T[:cw], grad_out.T[cw:]
    cot = in_order(
        lax.ppermute(jnp.where(odd, second, first), ALL, turn(0)),
        lax.ppermute(jnp.where(odd, first, second), ALL, turn(1)),
        0,
    )
    cot = lax.all_gather(
        jnp.concatenate([cot, jnp.pad(digits, ((0, 12), (0, 0)))], axis=0), "vocab"
    )
    digits = cot[:, fw : fw + 4].astype(jnp.int32)
    all_ids = 256 * digits[:, 0::2] + digits[:, 1::2]
    local_ids = (all_ids - v * entries).reshape(nv, 1, 2 * toks)

    shares = grad_products(weights, cot, nb, cw, 2 * fw)
    pieces, shares = lax.optimization_barrier((lookup(local_ids, table), shares))
    grads = lax.psum_scatter(
        shares.reshape(nb * 2 * fw, toks), "yhi", scatter_dimension=0, tiled=True
    ).astype(F32)
    pieces = lax.all_to_all(pieces, "vocab", 0, 0, tiled=True)
    cols = jnp.sum(pieces.astype(F32), axis=0).astype(BF16)
    first, second = cols[:, :toks], cols[:, toks:]
    embed = in_order(
        lax.ppermute(jnp.where(odd, second, first), ALL, swap_route(0)),
        lax.ppermute(jnp.where(odd, first, second), ALL, swap_route(1)),
        0,
    ).astype(F32)

    hid = hidden.T.astype(F32)
    gain_e, gain_h = gain_embed[:, None], gain_hidden[:, None]
    grad_left, grad_right = grads[:fw], grads[fw:]
    dn_embed, dn_hidden = grad_left * gain_e, grad_right * gain_h
    stats = jnp.stack(
        [
            jnp.sum(embed * embed, axis=0),
            jnp.sum(hid * hid, axis=0),
            jnp.sum(dn_embed * embed, axis=0),
            jnp.sum(dn_hidden * hid, axis=0),
        ]
    )
    stats = jnp.sum(gather(stats, "vocab", nv), axis=0)
    inv_embed = lax.rsqrt(stats[0] / full + EPS)[None]
    inv_hidden = lax.rsqrt(stats[1] / full + EPS)[None]
    norm_embed, norm_hidden = embed * inv_embed, hid * inv_hidden
    coef_embed = stats[2][None] * inv_embed / full
    coef_hidden = stats[3][None] * inv_hidden / full
    grad_embedded = (inv_embed * (dn_embed - norm_embed * coef_embed)).astype(BF16)
    grad_hidden = (inv_hidden * (dn_hidden - norm_hidden * coef_hidden)).astype(BF16)

    gains = jnp.concatenate(
        [jnp.sum(grad_left * norm_embed, axis=1), jnp.sum(grad_right * norm_hidden, axis=1)]
    )
    lines = -(-2 * fw // toks)
    gains = jnp.pad(gains, (0, lines * toks - 2 * fw)).reshape(lines, toks)
    gains = jnp.pad(gains, ((0, 16 - lines), (0, 0)))
    gains_high = gains.astype(BF16)
    gains_low = (gains - gains_high.astype(F32)).astype(BF16)
    normed = gather(
        jnp.concatenate(
            [
                (norm_embed * gain_e).astype(BF16),
                (norm_hidden * gain_h).astype(BF16),
                gains_high,
                gains_low,
            ],
            axis=0,
        ),
        "yhi",
        nb,
    )

    low, high = grad_embedded[:cw], grad_embedded[cw:]
    mine = in_order(
        lax.ppermute(jnp.where(odd, high, low), ALL, swap_back(0)),
        lax.ppermute(jnp.where(odd, low, high), ALL, swap_back(1)),
        0,
    )

    terms, weight_terms = out_products(weights, cot, normed, mine, cw, 2 * fw)
    terms = lax.all_to_all(terms, "vocab", 0, 0, tiled=True)
    grad_table = scatter(local_ids, terms, entries)

    terms = jnp.sum(terms[:, :fw].astype(F32), axis=0).astype(BF16)
    first, second = terms[:cw], terms[cw:]
    projected = in_order(
        lax.ppermute(jnp.where(odd, second, first), ALL, turn_back(0)),
        lax.ppermute(jnp.where(odd, first, second), ALL, turn_back(1)),
        0,
    )
    weight_terms = lax.psum_scatter(
        weight_terms.reshape(na * (cw + 16), 2 * fw), "z", scatter_dimension=0, tiled=True
    )
    grad_embed, grad_hid, grad_gains = finish(weight_terms, projected, cw, fw, lines)
    return (projected.T, grad_hidden.T, grad_table, grad_embed, grad_hid, grad_gains)


def solution(mesh):
    nv, nd = mesh.shape["vocab"], mesh.shape["dp"]
    nb = min(4, nd)
    split = Mesh(mesh.devices.reshape(nv, nd // nb, nb), ALL)
    rows = P(DP, "vocab")
    return jax.shard_map(
        per_device,
        mesh=split,
        in_specs=(
            P(DP),
            rows,
            rows,
            P("vocab"),
            P("vocab"),
            P("vocab", DP),
            P("vocab", DP),
            rows,
        ),
        out_specs=(rows, rows, rows, P("vocab", DP), P("vocab", DP), P(None, "vocab")),
        check_vma=False,
    )
```

```python
import functools

import jax
import jax.numpy as jnp
from jax import lax
from jax.experimental import pallas as pl
from jax.experimental.pallas import tpu as pltpu
from jax.sharding import Mesh
from jax.sharding import PartitionSpec as P

EPS = 1e-06
GROUPS = 8
BF16 = jnp.bfloat16
F32 = jnp.float32
DP = ("z", "yhi")
ALL = ("vocab", "z", "yhi")


def gather(x, axes, count):
    return lax.all_to_all(
        jnp.broadcast_to(x[None], (count,) + x.shape), axes, 0, 0, tiled=True
    )


def one_hot_of(ids, width):
    rows = lax.broadcasted_iota(jnp.int32, (width, ids.shape[1]), 0)
    return jnp.where(rows == ids % width, 1.0, 0.0).astype(BF16)


def group_of(ids, width):
    return lax.div(jnp.where(ids < 0, -width, ids), width)


def lookup_kernel(ids_ref, table_ref, out_ref):
    parts, _, rows = ids_ref.shape
    width = table_ref.shape[1]
    cols = table_ref.shape[0] // GROUPS
    ids = jnp.concatenate([ids_ref[i] for i in range(parts)], axis=1)
    picked = jnp.dot(
        table_ref[...], one_hot_of(ids, width), preferred_element_type=F32
    )
    group = group_of(ids, width)
    total = jnp.zeros((cols, ids.shape[1]), F32)
    for k in range(GROUPS):
        total = jnp.where(group == k, picked[k * cols : (k + 1) * cols], total)
    for i in range(parts):
        out_ref[i] = total[:, i * rows : (i + 1) * rows].astype(BF16)


def lookup(ids, table):
    blocks, _, rows = ids.shape
    cols, entries = table.shape
    width = entries // GROUPS
    parts = 4
    stacked = table.reshape(cols, GROUPS, width).transpose(1, 0, 2).reshape(cols * GROUPS, width)
    return pl.pallas_call(
        lookup_kernel,
        grid=(blocks // parts,),
        in_specs=[
            pl.BlockSpec((parts, 1, rows), lambda i: (i, 0, 0)),
            pl.BlockSpec((cols * GROUPS, width), lambda i: (0, 0)),
        ],
        out_specs=pl.BlockSpec((parts, cols, rows), lambda i: (i, 0, 0)),
        out_shape=jax.ShapeDtypeStruct((blocks, cols, rows), BF16),
        cost_estimate=pl.CostEstimate(
            flops=2 * blocks * rows * cols * entries,
            bytes_accessed=2 * cols * (entries + blocks * rows),
            transcendentals=0,
        ),
        compiler_params=pltpu.CompilerParams(vmem_limit_bytes=32 * 1024 * 1024),
    )(ids, stacked)


def scatter_kernel(ids_ref, rows_ref, out_ref):
    width = out_ref.shape[1] // GROUPS
    cols = out_ref.shape[0]
    parts = ids_ref.shape[0]
    ids = jnp.concatenate([ids_ref[i] for i in range(parts)], axis=1)
    values = jnp.concatenate(
        [rows_ref[i, j * cols : (j + 1) * cols] for i in range(parts) for j in range(2)], axis=1
    )
    group = group_of(ids, width)
    spread = jnp.concatenate(
        [values * jnp.where(group == k, 1.0, 0.0).astype(BF16) for k in range(GROUPS)], axis=0
    )
    sums = lax.dot_general(
        spread, one_hot_of(ids, width), (((1,), (1,)), ((), ())), preferred_element_type=F32
    )

    @pl.when(pl.program_id(0) == 0)
    def _():
        for k in range(GROUPS):
            out_ref[:, k * width : (k + 1) * width] = sums[k * cols : (k + 1) * cols]

    @pl.when(pl.program_id(0) > 0)
    def _():
        for k in range(GROUPS):
            out_ref[:, k * width : (k + 1) * width] += sums[k * cols : (k + 1) * cols]


def scatter(ids, values, entries):
    blocks, rows, toks = values.shape
    cols = rows // 2
    parts = 4
    return pl.pallas_call(
        scatter_kernel,
        grid=(blocks // parts,),
        in_specs=[
            pl.BlockSpec((parts, 1, 2 * toks), lambda i: (i, 0, 0)),
            pl.BlockSpec((parts, 2 * cols, toks), lambda i: (i, 0, 0)),
        ],
        out_specs=pl.BlockSpec((cols, entries), lambda i: (0, 0)),
        out_shape=jax.ShapeDtypeStruct((cols, entries), F32),
        cost_estimate=pl.CostEstimate(
            flops=4 * blocks * toks * cols * entries,
            bytes_accessed=cols * (4 * entries + 4 * blocks * toks),
            transcendentals=0,
        ),
        compiler_params=pltpu.CompilerParams(vmem_limit_bytes=32 * 1024 * 1024),
    )(ids, values)


def cot_columns(cot_ref, b, cw):
    half = b % 2 * cw
    return jnp.concatenate(
        [cot_ref[i, half : half + cw] for i in range(b // 2, cot_ref.shape[0], 2)], axis=0
    )


def grad_kernel(cw, weights_ref, cot_ref, out_ref):
    nb, feats, _ = out_ref.shape
    weights = jnp.concatenate(
        [weights_ref[a, :cw, :feats] for a in range(weights_ref.shape[0])], axis=0
    ).T
    for b in range(nb):
        out_ref[b] = jnp.dot(
            weights, cot_columns(cot_ref, b, cw), preferred_element_type=F32
        ).astype(BF16)


def grad_products(weights, cot, nb, cw, feats):
    na, toks = weights.shape[0], cot.shape[2]
    return pl.pallas_call(
        functools.partial(grad_kernel, cw),
        out_shape=jax.ShapeDtypeStruct((nb, feats, toks), BF16),
        cost_estimate=pl.CostEstimate(
            flops=2 * na * cw * feats * nb * toks,
            bytes_accessed=2 * (weights.size + cot.size + nb * feats * toks),
            transcendentals=0,
        ),
        compiler_params=pltpu.CompilerParams(vmem_limit_bytes=16 * 1024 * 1024),
    )(weights, cot)


def out_kernel(cw, feats, weights_ref, cot_ref, normed_ref, out_ref, sums_ref):
    na, nb = weights_ref.shape[0], normed_ref.shape[0]
    toks = normed_ref.shape[2]
    weights = jnp.concatenate([weights_ref[a, :cw, :feats] for a in range(na)], axis=0)
    for b in range(nb):
        terms = jnp.dot(weights, normed_ref[b, :feats], preferred_element_type=F32).astype(BF16)
        for a in range(na):
            half = b % 2 * cw
            out_ref[2 * a + b // 2, half : half + cw] = terms[a * cw : (a + 1) * cw]
    cot = jnp.concatenate([cot_columns(cot_ref, b, cw) for b in range(nb)], axis=1)
    normed = jnp.concatenate([normed_ref[b, :feats] for b in range(nb)], axis=1)
    sums = lax.dot_general(
        cot, normed, (((1,), (1,)), ((), ())), preferred_element_type=F32
    ).astype(BF16)
    gains = jnp.zeros((16, toks), F32)
    for b in range(nb):
        gains += normed_ref[b, feats : feats + 16].astype(F32)
        gains += normed_ref[b, feats + 16 : feats + 32].astype(F32)
    for a in range(na):
        sums_ref[a, :cw] = sums[a * cw : (a + 1) * cw]
        sums_ref[a, cw:] = jnp.zeros((16, feats), BF16)
        sums_ref[a, cw:, :toks] = gains.astype(BF16)


def out_products(weights, cot, normed, cw, feats):
    na, (nb, _, toks) = weights.shape[0], normed.shape
    return pl.pallas_call(
        functools.partial(out_kernel, cw, feats),
        out_shape=(
            jax.ShapeDtypeStruct((2 * na, 2 * cw, toks), BF16),
            jax.ShapeDtypeStruct((na, cw + 16, feats), BF16),
        ),
        cost_estimate=pl.CostEstimate(
            flops=4 * na * cw * feats * nb * toks,
            bytes_accessed=2 * (weights.size + 2 * cot.size + normed.size + na * cw * feats),
            transcendentals=0,
        ),
        compiler_params=pltpu.CompilerParams(vmem_limit_bytes=32 * 1024 * 1024),
    )(weights, cot, normed)


def finish_kernel(cw, fw, lines, sums_ref, done_ref, embed_ref, hidden_ref, gains_ref):
    toks = done_ref.shape[1]
    sums = sums_ref[...].astype(F32)
    turned = sums.T
    embed_ref[...] = turned[:fw, :cw]
    hidden_ref[...] = turned[fw:, :cw]
    gains = jnp.concatenate(
        [sums[cw + i : cw + i + 1, :toks] for i in range(lines)], axis=1
    )
    gains_ref[0:1, :] = gains[:, :fw]
    gains_ref[1:2, :] = gains[:, fw : 2 * fw]


def finish(sums, done, cw, fw, lines):
    return pl.pallas_call(
        functools.partial(finish_kernel, cw, fw, lines),
        out_shape=(
            jax.ShapeDtypeStruct((fw, cw), F32),
            jax.ShapeDtypeStruct((fw, cw), F32),
            jax.ShapeDtypeStruct((2, fw), F32),
        ),
        cost_estimate=pl.CostEstimate(
            flops=0, bytes_accessed=2 * sums.size + 8 * fw * cw, transcendentals=0
        ),
    )(sums, done)


def per_device(ids, hidden, table, gain_embed, gain_hidden, proj_embed, proj_hidden, grad_out):
    v = lax.axis_index("vocab")
    nv = lax.axis_size("vocab")
    na, nb = lax.axis_size("z"), lax.axis_size("yhi")
    nd = na * nb
    d = lax.axis_index("z") * nb + lax.axis_index("yhi")
    odd = d % 2 == 1
    toks, fw = hidden.shape
    cw, entries = table.shape
    full = fw * nv

    def swap_route(c):
        return [
            (i * nd + j, (j // 2) * nd + 2 * i + (j % 2 + c) % 2)
            for i in range(nv)
            for j in range(nd)
        ]

    def swap_back(c):
        return [(b, a) for a, b in swap_route(c)]

    def in_order(got0, got1, axis):
        return jnp.concatenate(
            [jnp.where(odd, got1, got0), jnp.where(odd, got0, got1)], axis=axis
        )

    def turn(c):
        return [
            (
                (2 * a2 + b1) * nd + a * nb + 2 * core + x,
                (2 * a2 + core) * nd + a * nb + 2 * b1 + (x + c) % 2,
            )
            for a2 in range(na)
            for b1 in range(2)
            for a in range(na)
            for core in range(2)
            for x in range(2)
        ]

    def turn_back(c):
        return [(b, a) for a, b in turn(c)]

    weights = jnp.concatenate([proj_embed, proj_hidden], axis=0).T
    weights = gather(weights, "z", na)

    digits = jnp.stack([ids // 256, ids % 256]).astype(BF16)
    digits = in_order(
        lax.ppermute(digits, ALL, swap_route(0)), lax.ppermute(digits, ALL, swap_route(1)), 0
    )
    first, second = grad_out.T[:cw], grad_out.T[cw:]
    cot = in_order(
        lax.ppermute(jnp.where(odd, second, first), ALL, turn(0)),
        lax.ppermute(jnp.where(odd, first, second), ALL, turn(1)),
        0,
    )
    cot = lax.all_gather(
        jnp.concatenate([cot, jnp.pad(digits, ((0, 12), (0, 0)))], axis=0), "vocab"
    )
    digits = cot[:, fw : fw + 4].astype(jnp.int32)
    all_ids = 256 * digits[:, 0::2] + digits[:, 1::2]
    local_ids = (all_ids - v * entries).reshape(nv, 1, 2 * toks)

    shares = grad_products(weights, cot, nb, cw, 2 * fw)
    pieces, shares = lax.optimization_barrier((lookup(local_ids, table), shares))
    grads = lax.psum_scatter(
        shares.reshape(nb * 2 * fw, toks), "yhi", scatter_dimension=0, tiled=True
    ).astype(F32)
    pieces = lax.all_to_all(pieces, "vocab", 0, 0, tiled=True)
    cols = jnp.sum(pieces.astype(F32), axis=0).astype(BF16)
    first, second = cols[:, :toks], cols[:, toks:]
    embed = in_order(
        lax.ppermute(jnp.where(odd, second, first), ALL, swap_route(0)),
        lax.ppermute(jnp.where(odd, first, second), ALL, swap_route(1)),
        0,
    ).astype(F32)

    hid = hidden.T.astype(F32)
    gain_e, gain_h = gain_embed[:, None], gain_hidden[:, None]
    grad_left, grad_right = grads[:fw], grads[fw:]
    dn_embed, dn_hidden = grad_left * gain_e, grad_right * gain_h
    stats = jnp.stack(
        [
            jnp.sum(embed * embed, axis=0),
            jnp.sum(hid * hid, axis=0),
            jnp.sum(dn_embed * embed, axis=0),
            jnp.sum(dn_hidden * hid, axis=0),
        ]
    )
    stats = jnp.sum(gather(stats, "vocab", nv), axis=0)
    inv_embed = lax.rsqrt(stats[0] / full + EPS)[None]
    inv_hidden = lax.rsqrt(stats[1] / full + EPS)[None]
    norm_embed, norm_hidden = embed * inv_embed, hid * inv_hidden
    coef_embed = stats[2][None] * inv_embed / full
    coef_hidden = stats[3][None] * inv_hidden / full
    grad_embedded = (inv_embed * (dn_embed - norm_embed * coef_embed)).astype(BF16)
    grad_hidden = (inv_hidden * (dn_hidden - norm_hidden * coef_hidden)).astype(BF16)

    gains = jnp.concatenate(
        [jnp.sum(grad_left * norm_embed, axis=1), jnp.sum(grad_right * norm_hidden, axis=1)]
    )
    lines = -(-2 * fw // toks)
    gains = jnp.pad(gains, (0, lines * toks - 2 * fw)).reshape(lines, toks)
    gains = jnp.pad(gains, ((0, 16 - lines), (0, 0)))
    gains_high = gains.astype(BF16)
    gains_low = (gains - gains_high.astype(F32)).astype(BF16)
    normed = gather(
        jnp.concatenate(
            [
                (norm_embed * gain_e).astype(BF16),
                (norm_hidden * gain_h).astype(BF16),
                gains_high,
                gains_low,
            ],
            axis=0,
        ),
        "yhi",
        nb,
    )

    low, high = grad_embedded[:cw], grad_embedded[cw:]
    mine = in_order(
        lax.ppermute(jnp.where(odd, high, low), ALL, swap_back(0)),
        lax.ppermute(jnp.where(odd, low, high), ALL, swap_back(1)),
        0,
    )

    normed, mine = lax.optimization_barrier((normed, mine))
    terms, weight_terms = out_products(weights, cot, normed, cw, 2 * fw)
    mine, weight_terms = lax.optimization_barrier((mine, weight_terms))
    grad_table = scatter(local_ids, lax.all_gather(mine, "vocab"), entries)

    terms = lax.all_to_all(terms, "vocab", 0, 0, tiled=True)
    terms = jnp.sum(terms.astype(F32), axis=0).astype(BF16)
    first, second = terms[:cw], terms[cw:]
    projected = in_order(
        lax.ppermute(jnp.where(odd, second, first), ALL, turn_back(0)),
        lax.ppermute(jnp.where(odd, first, second), ALL, turn_back(1)),
        0,
    )
    weight_terms = lax.psum_scatter(
        weight_terms.reshape(na * (cw + 16), 2 * fw), "z", scatter_dimension=0, tiled=True
    )
    grad_embed, grad_hid, grad_gains = finish(weight_terms, projected, cw, fw, lines)
    return (projected.T, grad_hidden.T, grad_table, grad_embed, grad_hid, grad_gains)


def solution(mesh):
    nv, nd = mesh.shape["vocab"], mesh.shape["dp"]
    nb = min(4, nd)
    split = Mesh(mesh.devices.reshape(nv, nd // nb, nb), ALL)
    rows = P(DP, "vocab")
    return jax.shard_map(
        per_device,
        mesh=split,
        in_specs=(
            P(DP),
            rows,
            rows,
            P("vocab"),
            P("vocab"),
            P("vocab", DP),
            P("vocab", DP),
            rows,
        ),
        out_specs=(rows, rows, rows, P("vocab", DP), P("vocab", DP), P(None, "vocab")),
        check_vma=False,
    )
```

```python
import functools

import jax
import jax.numpy as jnp
from jax import lax
from jax.experimental import pallas as pl
from jax.experimental.pallas import tpu as pltpu
from jax.sharding import Mesh
from jax.sharding import PartitionSpec as P

EPS = 1e-06
GROUPS = 8
BF16 = jnp.bfloat16
F32 = jnp.float32
DP = ("z", "yhi")
ALL = ("chip", "core", "z", "yhi")
VOCAB = ("chip", "core")


def gather(x, axes, count):
    return lax.all_to_all(
        jnp.broadcast_to(x[None], (count,) + x.shape), axes, 0, 0, tiled=True
    )


def one_hot_of(ids, width):
    rows = lax.broadcasted_iota(jnp.int32, (width, ids.shape[1]), 0)
    return jnp.where(rows == ids % width, 1.0, 0.0).astype(BF16)


def group_of(ids, width):
    return lax.div(jnp.where(ids < 0, -width, ids), width)


def lookup_kernel(ids_ref, table_ref, out_ref):
    parts, _, rows = ids_ref.shape
    width = table_ref.shape[1]
    cols = table_ref.shape[0] // GROUPS
    ids = jnp.concatenate([ids_ref[i] for i in range(parts)], axis=1)
    picked = jnp.dot(
        table_ref[...], one_hot_of(ids, width), preferred_element_type=F32
    )
    group = group_of(ids, width)
    total = jnp.zeros((cols, ids.shape[1]), F32)
    for k in range(GROUPS):
        total = jnp.where(group == k, picked[k * cols : (k + 1) * cols], total)
    for i in range(parts):
        out_ref[i] = total[:, i * rows : (i + 1) * rows].astype(BF16)


def lookup(ids, table):
    blocks, _, rows = ids.shape
    cols, entries = table.shape
    width = entries // GROUPS
    parts = 4
    stacked = table.reshape(cols, GROUPS, width).transpose(1, 0, 2).reshape(cols * GROUPS, width)
    return pl.pallas_call(
        lookup_kernel,
        grid=(blocks // parts,),
        in_specs=[
            pl.BlockSpec((parts, 1, rows), lambda i: (i, 0, 0)),
            pl.BlockSpec((cols * GROUPS, width), lambda i: (0, 0)),
        ],
        out_specs=pl.BlockSpec((parts, cols, rows), lambda i: (i, 0, 0)),
        out_shape=jax.ShapeDtypeStruct((blocks, cols, rows), BF16),
        cost_estimate=pl.CostEstimate(
            flops=2 * blocks * rows * cols * entries,
            bytes_accessed=2 * cols * (entries + blocks * rows),
            transcendentals=0,
        ),
        compiler_params=pltpu.CompilerParams(vmem_limit_bytes=32 * 1024 * 1024),
    )(ids, stacked)


def scatter_kernel(ids_ref, own_ref, other_ref, out_ref, done_ref):
    width = out_ref.shape[1] // GROUPS
    cols = out_ref.shape[0]
    parts = ids_ref.shape[0]
    step = pl.program_id(0)
    own = 2 * step < pl.num_programs(0)
    ids = jnp.concatenate([ids_ref[i] for i in range(parts)], axis=1)
    values = jnp.concatenate(
        [
            jnp.where(
                own, own_ref[i, j * cols : (j + 1) * cols], other_ref[i, j * cols : (j + 1) * cols]
            )
            for i in range(parts)
            for j in range(2)
        ],
        axis=1,
    )
    group = group_of(ids, width)
    spread = jnp.concatenate(
        [values * jnp.where(group == k, 1.0, 0.0).astype(BF16) for k in range(GROUPS)], axis=0
    )
    sums = lax.dot_general(
        spread, one_hot_of(ids, width), (((1,), (1,)), ((), ())), preferred_element_type=F32
    )
    done_ref[...] = jnp.zeros_like(done_ref)

    @pl.when(pl.program_id(0) == 0)
    def _():
        for k in range(GROUPS):
            out_ref[:, k * width : (k + 1) * width] = sums[k * cols : (k + 1) * cols]

    @pl.when(pl.program_id(0) > 0)
    def _():
        for k in range(GROUPS):
            out_ref[:, k * width : (k + 1) * width] += sums[k * cols : (k + 1) * cols]


def scatter(ids, own, other, entries):
    blocks, rows, toks = own.shape
    cols = rows // 2
    parts = 4
    half = blocks // parts
    return pl.pallas_call(
        scatter_kernel,
        grid=(2 * half,),
        in_specs=[
            pl.BlockSpec((parts, 1, 2 * toks), lambda i: (i, 0, 0)),
            pl.BlockSpec((parts, 2 * cols, toks), lambda i: (jnp.minimum(i, half - 1), 0, 0)),
            pl.BlockSpec((parts, 2 * cols, toks), lambda i: (jnp.maximum(i - half, 0), 0, 0)),
        ],
        out_specs=(
            pl.BlockSpec((cols, entries), lambda i: (0, 0)),
            pl.BlockSpec((8, 128), lambda i: (0, 0)),
        ),
        out_shape=(
            jax.ShapeDtypeStruct((cols, entries), F32),
            jax.ShapeDtypeStruct((8, 128), F32),
        ),
        cost_estimate=pl.CostEstimate(
            flops=8 * blocks * toks * cols * entries,
            bytes_accessed=cols * (4 * entries + 8 * blocks * toks),
            transcendentals=0,
        ),
        compiler_params=pltpu.CompilerParams(vmem_limit_bytes=32 * 1024 * 1024),
    )(ids, own, other)


def cot_columns(core, own_ref, other_ref, b, cw):
    half = b % 2 * cw
    own = core == b // 2
    return jnp.concatenate(
        [
            jnp.where(own, own_ref[i, half : half + cw], other_ref[i, half : half + cw])
            for i in range(own_ref.shape[0])
        ],
        axis=0,
    )


def grad_kernel(cw, place_ref, weights_ref, own_ref, other_ref, out_ref):
    nb, feats, _ = out_ref.shape
    weights = jnp.concatenate([weights_ref[a] for a in range(weights_ref.shape[0])], axis=0).T
    for b in range(nb):
        share = jnp.dot(
            weights,
            cot_columns(place_ref[0], own_ref, other_ref, b, cw),
            preferred_element_type=F32,
        )
        out_ref[lax.rem(b + nb - place_ref[1], nb)] = share.astype(BF16)


def grad_products(place, weights, own, other, nb):
    na, cw, feats = weights.shape
    toks = own.shape[2]
    whole = pl.BlockSpec(memory_space=pltpu.VMEM)
    return pl.pallas_call(
        functools.partial(grad_kernel, cw),
        in_specs=[pl.BlockSpec(memory_space=pltpu.SMEM), whole, whole, whole],
        out_shape=jax.ShapeDtypeStruct((nb, feats, toks), BF16),
        cost_estimate=pl.CostEstimate(
            flops=2 * na * cw * feats * nb * toks,
            bytes_accessed=2 * (weights.size + 2 * own.size + nb * feats * toks),
            transcendentals=0,
        ),
        compiler_params=pltpu.CompilerParams(vmem_limit_bytes=16 * 1024 * 1024),
    )(place, weights, own, other)


def out_kernel(
    place_ref, weights_ref, own_ref, other_ref, normed_ref, keep_ref, send_ref, top_ref, low_ref
):
    na, cw, feats = weights_ref.shape
    nb, _, toks = normed_ref.shape
    core = place_ref[0]
    weights = jnp.concatenate([weights_ref[a] for a in range(na)], axis=0)
    terms = [
        jnp.dot(weights, normed_ref[b, :feats], preferred_element_type=F32) for b in range(nb)
    ]
    for x in range(2):
        keep = jnp.where(core == 0, terms[x], terms[x + 2]).astype(BF16)
        send = jnp.where(core == 0, terms[x + 2], terms[x]).astype(BF16)
        for a in range(na):
            keep_ref[a, x * cw : (x + 1) * cw] = keep[a * cw : (a + 1) * cw]
            send_ref[a, x * cw : (x + 1) * cw] = send[a * cw : (a + 1) * cw]
    cot = jnp.concatenate(
        [cot_columns(core, own_ref, other_ref, b, cw) for b in range(nb)], axis=1
    )
    normed = jnp.concatenate([normed_ref[b, :feats] for b in range(nb)], axis=1)
    sums = lax.dot_general(
        cot, normed, (((1,), (1,)), ((), ())), preferred_element_type=F32
    ).astype(BF16)
    gains = jnp.zeros((16, toks), F32)
    for b in range(nb):
        gains += normed_ref[b, feats : feats + 16].astype(F32)
        gains += normed_ref[b, feats + 16 : feats + 32].astype(F32)
    half = top_ref.shape[1]
    for a in range(na):
        top_ref[a] = sums[a * cw : a * cw + half]
        low_ref[a, : cw - half] = sums[a * cw + half : (a + 1) * cw]
        low_ref[a, cw - half :] = jnp.zeros((16, feats), BF16)
        low_ref[a, cw - half :, :toks] = gains.astype(BF16)


def out_products(place, weights, own, other, normed):
    na, cw, feats = weights.shape
    nb, _, toks = normed.shape
    whole = pl.BlockSpec(memory_space=pltpu.VMEM)
    return pl.pallas_call(
        out_kernel,
        in_specs=[pl.BlockSpec(memory_space=pltpu.SMEM), whole, whole, whole, whole],
        out_shape=(
            jax.ShapeDtypeStruct((na, 2 * cw, toks), BF16),
            jax.ShapeDtypeStruct((na, 2 * cw, toks), BF16),
            jax.ShapeDtypeStruct((na, (cw + 16) // 2, feats), BF16),
            jax.ShapeDtypeStruct((na, (cw + 16) // 2, feats), BF16),
        ),
        cost_estimate=pl.CostEstimate(
            flops=4 * na * cw * feats * nb * toks,
            bytes_accessed=2 * (weights.size + 4 * own.size + normed.size + na * cw * feats),
            transcendentals=0,
        ),
        compiler_params=pltpu.CompilerParams(vmem_limit_bytes=32 * 1024 * 1024),
    )(place, weights, own, other, normed)


def finish_kernel(cw, toks, lines, top_ref, low_ref, done_ref, embed_ref, hidden_ref, gains_ref):
    fw = embed_ref.shape[0]
    sums = jnp.concatenate([top_ref[...].astype(F32), low_ref[...].astype(F32)], axis=0)
    turned = sums.T
    embed_ref[...] = turned[:fw, :cw]
    hidden_ref[...] = turned[fw:, :cw]
    gains = jnp.concatenate(
        [sums[cw + i : cw + i + 1, :toks] for i in range(lines)], axis=1
    )
    gains_ref[0:1, :] = gains[:, :fw]
    gains_ref[1:2, :] = gains[:, fw : 2 * fw]


def finish(top, low, done, cw, toks, lines):
    fw = top.shape[1] // 2
    return pl.pallas_call(
        functools.partial(finish_kernel, cw, toks, lines),
        out_shape=(
            jax.ShapeDtypeStruct((fw, cw), F32),
            jax.ShapeDtypeStruct((fw, cw), F32),
            jax.ShapeDtypeStruct((2, fw), F32),
        ),
        cost_estimate=pl.CostEstimate(
            flops=0, bytes_accessed=4 * top.size + 8 * fw * cw, transcendentals=0
        ),
    )(top, low, done)


def per_device(ids, hidden, table, gain_embed, gain_hidden, proj_embed, proj_hidden, grad_out):
    core = lax.axis_index("core")
    v = 2 * lax.axis_index("chip") + core
    nc = lax.axis_size("chip")
    nv = 2 * nc
    na, nb = lax.axis_size("z"), lax.axis_size("yhi")
    nd = na * nb
    yhi = lax.axis_index("yhi")
    d = lax.axis_index("z") * nb + yhi
    place = jnp.stack([core, yhi]).astype(jnp.int32)
    odd = d % 2 == 1
    toks, fw = hidden.shape
    cw, entries = table.shape
    full = fw * nv

    def swap_route(c):
        return [
            (i * nd + j, (j // 2) * nd + 2 * i + (j % 2 + c) % 2)
            for i in range(nv)
            for j in range(nd)
        ]

    def swap_back(c):
        return [(b, a) for a, b in swap_route(c)]

    def in_order(got0, got1, axis):
        return jnp.concatenate(
            [jnp.where(odd, got1, got0), jnp.where(odd, got0, got1)], axis=axis
        )

    def turn(c):
        return [
            (
                (2 * a2 + b1) * nd + a * nb + 2 * core + x,
                (2 * a2 + core) * nd + a * nb + 2 * b1 + (x + c) % 2,
            )
            for a2 in range(na)
            for b1 in range(2)
            for a in range(na)
            for core in range(2)
            for x in range(2)
        ]

    def turn_back(c):
        return [(b, a) for a, b in turn(c)]

    def flip(x):
        return lax.ppermute(x, "core", [(0, 1), (1, 0)])

    weights = jnp.concatenate([proj_embed, proj_hidden], axis=0).T
    weights = gather(weights, "z", na)

    digits = jnp.stack([ids // 256, ids % 256]).astype(BF16)
    digits = in_order(
        lax.ppermute(digits, ALL, swap_route(0)), lax.ppermute(digits, ALL, swap_route(1)), 0
    )
    first, second = grad_out.T[:cw], grad_out.T[cw:]
    cot = in_order(
        lax.ppermute(jnp.where(odd, second, first), ALL, turn(0)),
        lax.ppermute(jnp.where(odd, first, second), ALL, turn(1)),
        0,
    )
    cot = jnp.concatenate([cot, jnp.pad(digits, ((0, 12), (0, 0)))], axis=0)
    cot, weights = lax.optimization_barrier((cot, weights))
    own = gather(cot, "chip", nc)
    other = flip(own)

    def ids_of(cot):
        digits = cot[:, fw : fw + 4].astype(jnp.int32)
        all_ids = 256 * digits[:, 0::2] + digits[:, 1::2]
        return (all_ids - v * entries).reshape(nc, 1, 2 * toks)

    own_ids, other_ids = ids_of(own), ids_of(other)

    shares = grad_products(place, weights, own, other, nb)
    grads = shares[0].astype(F32)
    for k in range(1, nb):
        grads += lax.ppermute(
            shares[k], "yhi", [(i, (i + k) % nb) for i in range(nb)]
        ).astype(F32)

    pieces = lookup(own_ids, table) + flip(lookup(other_ids, table))
    pieces = lax.all_to_all(pieces, "chip", 0, 0, tiled=True)
    cols = jnp.sum(pieces.astype(F32), axis=0).astype(BF16)
    first, second = cols[:, :toks], cols[:, toks:]
    embed = in_order(
        lax.ppermute(jnp.where(odd, second, first), ALL, swap_route(0)),
        lax.ppermute(jnp.where(odd, first, second), ALL, swap_route(1)),
        0,
    ).astype(F32)

    hid = hidden.T.astype(F32)
    gain_e, gain_h = gain_embed[:, None], gain_hidden[:, None]
    grad_left, grad_right = grads[:fw], grads[fw:]
    dn_embed, dn_hidden = grad_left * gain_e, grad_right * gain_h
    stats = jnp.stack(
        [
            jnp.sum(embed * embed, axis=0),
            jnp.sum(hid * hid, axis=0),
            jnp.sum(dn_embed * embed, axis=0),
            jnp.sum(dn_hidden * hid, axis=0),
        ]
    )
    stats = jnp.sum(gather(stats + flip(stats), "chip", nc), axis=0)
    inv_embed = lax.rsqrt(stats[0] / full + EPS)[None]
    inv_hidden = lax.rsqrt(stats[1] / full + EPS)[None]
    norm_embed, norm_hidden = embed * inv_embed, hid * inv_hidden
    coef_embed = stats[2][None] * inv_embed / full
    coef_hidden = stats[3][None] * inv_hidden / full
    grad_embedded = (inv_embed * (dn_embed - norm_embed * coef_embed)).astype(BF16)
    grad_hidden = (inv_hidden * (dn_hidden - norm_hidden * coef_hidden)).astype(BF16)

    gains = jnp.concatenate(
        [jnp.sum(grad_left * norm_embed, axis=1), jnp.sum(grad_right * norm_hidden, axis=1)]
    )
    lines = -(-2 * fw // toks)
    gains = jnp.pad(gains, (0, lines * toks - 2 * fw)).reshape(lines, toks)
    gains = jnp.pad(gains, ((0, 16 - lines), (0, 0)))
    gains_high = gains.astype(BF16)
    gains_low = (gains - gains_high.astype(F32)).astype(BF16)
    normed = gather(
        jnp.concatenate(
            [
                (norm_embed * gain_e).astype(BF16),
                (norm_hidden * gain_h).astype(BF16),
                gains_high,
                gains_low,
            ],
            axis=0,
        ),
        "yhi",
        nb,
    )

    low, high = grad_embedded[:cw], grad_embedded[cw:]
    mine = in_order(
        lax.ppermute(jnp.where(odd, high, low), ALL, swap_back(0)),
        lax.ppermute(jnp.where(odd, low, high), ALL, swap_back(1)),
        0,
    )

    normed, mine = lax.optimization_barrier((normed, mine))
    keep, send, top, low_half = out_products(place, weights, own, other, normed)
    terms = (keep.astype(F32) + flip(send).astype(F32)).astype(BF16)
    mine = jnp.broadcast_to(mine[None], (nc,) + mine.shape)
    both = lax.all_to_all(
        jnp.concatenate([terms, mine], axis=1), "chip", 0, 0, tiled=True
    )
    own_rows = both[:, fw:]
    grad_table, done = scatter(
        jnp.concatenate([own_ids, other_ids], axis=0), own_rows, flip(own_rows), entries
    )

    terms = jnp.sum(both[:, :fw].astype(F32), axis=0).astype(BF16)
    first, second = terms[:cw], terms[cw:]
    projected = in_order(
        lax.ppermute(jnp.where(odd, second, first), ALL, turn_back(0)),
        lax.ppermute(jnp.where(odd, first, second), ALL, turn_back(1)),
        0,
    )
    top, low_half = (
        lax.psum_scatter(x.reshape(-1, 2 * fw), "z", scatter_dimension=0, tiled=True)
        for x in (top, low_half)
    )
    grad_embed, grad_hid, grad_gains = finish(top, low_half, done, cw, toks, lines)
    return (projected.T, grad_hidden.T, grad_table, grad_embed, grad_hid, grad_gains)


def solution(mesh):
    nv, nd = mesh.shape["vocab"], mesh.shape["dp"]
    nb = min(4, nd)
    split = Mesh(mesh.devices.reshape(nv // 2, 2, nd // nb, nb), ALL)
    rows = P(DP, VOCAB)
    return jax.shard_map(
        per_device,
        mesh=split,
        in_specs=(
            P(DP),
            rows,
            rows,
            P(VOCAB),
            P(VOCAB),
            P(VOCAB, DP),
            P(VOCAB, DP),
            rows,
        ),
        out_specs=(rows, rows, rows, P(VOCAB, DP), P(VOCAB, DP), P(None, VOCAB)),
        check_vma=False,
    )
```

```python
import functools

import jax
import jax.numpy as jnp
from jax import lax
from jax.experimental import pallas as pl
from jax.experimental.pallas import tpu as pltpu
from jax.sharding import Mesh
from jax.sharding import PartitionSpec as P

EPS = 1e-06
GROUPS = 8
PAD_ROWS = 80
BF16 = jnp.bfloat16
F32 = jnp.float32
DP = ("z", "yhi")
ALL = ("chip", "core", "z", "yhi")
VOCAB = ("chip", "core")


def gather(x, axes, count):
    return lax.all_to_all(
        jnp.broadcast_to(x[None], (count,) + x.shape), axes, 0, 0, tiled=True
    )


def one_hot_of(ids, width):
    rows = lax.broadcasted_iota(jnp.int32, (width, ids.shape[1]), 0)
    return jnp.where(rows == ids % width, 1.0, 0.0).astype(BF16)


def group_of(ids, width):
    return lax.div(jnp.where(ids < 0, -width, ids), width)


def lookup_kernel(ids_ref, table_ref, out_ref):
    parts, _, rows = ids_ref.shape
    width = table_ref.shape[1]
    cols = table_ref.shape[0] // GROUPS
    ids = jnp.concatenate([ids_ref[i] for i in range(parts)], axis=1)
    picked = jnp.dot(
        table_ref[...], one_hot_of(ids, width), preferred_element_type=F32
    )
    group = group_of(ids, width)
    total = jnp.zeros((cols, ids.shape[1]), F32)
    for k in range(GROUPS):
        total = jnp.where(group == k, picked[k * cols : (k + 1) * cols], total)
    for i in range(parts):
        out_ref[i] = total[:, i * rows : (i + 1) * rows].astype(BF16)


def lookup(ids, table):
    blocks, _, rows = ids.shape
    cols, entries = table.shape
    width = entries // GROUPS
    parts = 4
    stacked = table.reshape(cols, GROUPS, width).transpose(1, 0, 2).reshape(cols * GROUPS, width)
    return pl.pallas_call(
        lookup_kernel,
        grid=(blocks // parts,),
        in_specs=[
            pl.BlockSpec((parts, 1, rows), lambda i: (i, 0, 0)),
            pl.BlockSpec((cols * GROUPS, width), lambda i: (0, 0)),
        ],
        out_specs=pl.BlockSpec((parts, cols, rows), lambda i: (i, 0, 0)),
        out_shape=jax.ShapeDtypeStruct((blocks, cols, rows), BF16),
        cost_estimate=pl.CostEstimate(
            flops=2 * blocks * rows * cols * entries,
            bytes_accessed=2 * cols * (entries + blocks * rows),
            transcendentals=0,
        ),
        compiler_params=pltpu.CompilerParams(vmem_limit_bytes=32 * 1024 * 1024),
    )(ids, stacked)


def scatter_kernel(ids_ref, own_ref, other_ref, out_ref, done_ref):
    width = out_ref.shape[1] // GROUPS
    cols = out_ref.shape[0]
    parts = ids_ref.shape[0]
    step = pl.program_id(0)
    own = 2 * step < pl.num_programs(0)
    ids = jnp.concatenate([ids_ref[i] for i in range(parts)], axis=1)
    values = jnp.concatenate(
        [
            jnp.where(
                own, own_ref[i, j * cols : (j + 1) * cols], other_ref[i, j * cols : (j + 1) * cols]
            )
            for i in range(parts)
            for j in range(2)
        ],
        axis=1,
    )
    group = group_of(ids, width)
    spread = jnp.concatenate(
        [values * jnp.where(group == k, 1.0, 0.0).astype(BF16) for k in range(GROUPS)], axis=0
    )
    sums = lax.dot_general(
        spread, one_hot_of(ids, width), (((1,), (1,)), ((), ())), preferred_element_type=F32
    )
    done_ref[...] = jnp.zeros_like(done_ref)

    @pl.when(pl.program_id(0) == 0)
    def _():
        for k in range(GROUPS):
            out_ref[:, k * width : (k + 1) * width] = sums[k * cols : (k + 1) * cols]

    @pl.when(pl.program_id(0) > 0)
    def _():
        for k in range(GROUPS):
            out_ref[:, k * width : (k + 1) * width] += sums[k * cols : (k + 1) * cols]


def scatter(ids, own, other, entries):
    blocks, rows, toks = own.shape
    cols = rows // 2
    parts = 4
    half = blocks // parts
    return pl.pallas_call(
        scatter_kernel,
        grid=(2 * half,),
        in_specs=[
            pl.BlockSpec((parts, 1, 2 * toks), lambda i: (i, 0, 0)),
            pl.BlockSpec((parts, 2 * cols, toks), lambda i: (jnp.minimum(i, half - 1), 0, 0)),
            pl.BlockSpec((parts, 2 * cols, toks), lambda i: (jnp.maximum(i - half, 0), 0, 0)),
        ],
        out_specs=(
            pl.BlockSpec((cols, entries), lambda i: (0, 0)),
            pl.BlockSpec((8, 128), lambda i: (0, 0)),
        ),
        out_shape=(
            jax.ShapeDtypeStruct((cols, entries), F32),
            jax.ShapeDtypeStruct((8, 128), F32),
        ),
        cost_estimate=pl.CostEstimate(
            flops=0,
            bytes_accessed=0,
            transcendentals=0,
        ),
        compiler_params=pltpu.CompilerParams(vmem_limit_bytes=32 * 1024 * 1024),
    )(ids, own, other)


def cot_columns(core, own_ref, other_ref, b, cw):
    half = b % 2 * cw
    own = core == b // 2
    return jnp.concatenate(
        [
            jnp.where(own, own_ref[i, half : half + cw], other_ref[i, half : half + cw])
            for i in range(own_ref.shape[0])
        ],
        axis=0,
    )


def grad_kernel(cw, place_ref, weights_ref, own_ref, other_ref, out_ref):
    nb, feats, _ = out_ref.shape
    weights = jnp.concatenate([weights_ref[a] for a in range(weights_ref.shape[0])], axis=0).T
    for b in range(nb):
        share = jnp.dot(
            weights,
            cot_columns(place_ref[0], own_ref, other_ref, b, cw),
            preferred_element_type=F32,
        )
        out_ref[lax.rem(b + nb - place_ref[1], nb)] = share.astype(BF16)


def grad_products(place, weights, own, other, nb):
    na, cw, feats = weights.shape
    toks = own.shape[2]
    whole = pl.BlockSpec(memory_space=pltpu.VMEM)
    return pl.pallas_call(
        functools.partial(grad_kernel, cw),
        in_specs=[pl.BlockSpec(memory_space=pltpu.SMEM), whole, whole, whole],
        out_shape=jax.ShapeDtypeStruct((nb, feats, toks), BF16),
        cost_estimate=pl.CostEstimate(
            flops=2 * na * cw * feats * nb * toks,
            bytes_accessed=2 * (weights.size + 2 * own.size + nb * feats * toks),
            transcendentals=0,
        ),
        compiler_params=pltpu.CompilerParams(vmem_limit_bytes=16 * 1024 * 1024),
    )(place, weights, own, other)


def out_kernel(
    place_ref, weights_ref, own_ref, other_ref, normed_ref, keep_ref, send_ref, sums_ref
):
    na, cw, feats = weights_ref.shape
    nb, _, toks = normed_ref.shape
    core = place_ref[0]
    weights = jnp.concatenate([weights_ref[a] for a in range(na)], axis=0)
    terms = [
        jnp.dot(weights, normed_ref[b, :feats], preferred_element_type=F32) for b in range(nb)
    ]
    for x in range(2):
        keep = jnp.where(core == 0, terms[x], terms[x + 2]).astype(BF16)
        send = jnp.where(core == 0, terms[x + 2], terms[x]).astype(BF16)
        for a in range(na):
            keep_ref[a, x * cw : (x + 1) * cw] = keep[a * cw : (a + 1) * cw]
            send_ref[a, x * cw : (x + 1) * cw] = send[a * cw : (a + 1) * cw]
    cot = jnp.concatenate(
        [cot_columns(core, own_ref, other_ref, b, cw) for b in range(nb)], axis=1
    )
    normed = jnp.concatenate([normed_ref[b, :feats] for b in range(nb)], axis=1)
    sums = lax.dot_general(
        cot, normed, (((1,), (1,)), ((), ())), preferred_element_type=F32
    ).astype(BF16)
    gains = jnp.zeros((16, toks), F32)
    for b in range(nb):
        gains += normed_ref[b, feats : feats + 16].astype(F32)
        gains += normed_ref[b, feats + 16 : feats + 32].astype(F32)
    for a in range(na):
        sums_ref[a, :cw] = sums[a * cw : (a + 1) * cw]
        sums_ref[a, cw:] = jnp.zeros((PAD_ROWS, feats), BF16)
        sums_ref[a, cw : cw + 16, :toks] = gains.astype(BF16)


def out_products(place, weights, own, other, normed):
    na, cw, feats = weights.shape
    nb, _, toks = normed.shape
    whole = pl.BlockSpec(memory_space=pltpu.VMEM)
    return pl.pallas_call(
        out_kernel,
        in_specs=[pl.BlockSpec(memory_space=pltpu.SMEM), whole, whole, whole, whole],
        out_shape=(
            jax.ShapeDtypeStruct((na, 2 * cw, toks), BF16),
            jax.ShapeDtypeStruct((na, 2 * cw, toks), BF16),
            jax.ShapeDtypeStruct((na, cw + PAD_ROWS, feats), BF16),
        ),
        cost_estimate=pl.CostEstimate(
            flops=4 * na * cw * feats * nb * toks,
            bytes_accessed=2 * (weights.size + 4 * own.size + normed.size + na * cw * feats),
            transcendentals=0,
        ),
        compiler_params=pltpu.CompilerParams(vmem_limit_bytes=32 * 1024 * 1024),
    )(place, weights, own, other, normed)


def finish_kernel(
    lines, place_ref, sums_ref, got0_ref, got1_ref, done_ref, out_ref, embed_ref, hidden_ref, gains_ref
):
    fw, cw = embed_ref.shape
    toks = out_ref.shape[1]
    odd = lax.rem(place_ref[1], 2) == 1
    out_ref[:cw] = jnp.where(odd, got1_ref[...], got0_ref[...])
    out_ref[cw:] = jnp.where(odd, got0_ref[...], got1_ref[...])
    sums = sums_ref[...].astype(F32)
    turned = sums[:cw].T
    embed_ref[...] = turned[:fw]
    hidden_ref[...] = turned[fw:]
    gains = jnp.concatenate(
        [sums[cw + i : cw + i + 1, :toks] for i in range(lines)], axis=1
    )
    gains_ref[0:1, :] = gains[:, :fw]
    gains_ref[1:2, :] = gains[:, fw : 2 * fw]


def finish(place, sums, got0, got1, done, lines):
    fw = sums.shape[1] // 2
    cw, toks = got0.shape
    whole = pl.BlockSpec(memory_space=pltpu.VMEM)
    return pl.pallas_call(
        functools.partial(finish_kernel, lines),
        in_specs=[pl.BlockSpec(memory_space=pltpu.SMEM), whole, whole, whole, whole],
        out_shape=(
            jax.ShapeDtypeStruct((2 * cw, toks), BF16),
            jax.ShapeDtypeStruct((fw, cw), F32),
            jax.ShapeDtypeStruct((fw, cw), F32),
            jax.ShapeDtypeStruct((2, fw), F32),
        ),
        cost_estimate=pl.CostEstimate(
            flops=0, bytes_accessed=2 * sums.size + 8 * fw * cw, transcendentals=0
        ),
    )(place, sums, got0, got1, done)


def per_device(ids, hidden, table, gain_embed, gain_hidden, proj_embed, proj_hidden, grad_out):
    core = lax.axis_index("core")
    v = 2 * lax.axis_index("chip") + core
    nc = lax.axis_size("chip")
    nv = 2 * nc
    na, nb = lax.axis_size("z"), lax.axis_size("yhi")
    nd = na * nb
    yhi = lax.axis_index("yhi")
    d = lax.axis_index("z") * nb + yhi
    place = jnp.stack([core, yhi]).astype(jnp.int32)
    odd = d % 2 == 1
    toks, fw = hidden.shape
    cw, entries = table.shape
    full = fw * nv

    def swap_route(c):
        return [
            (i * nd + j, (j // 2) * nd + 2 * i + (j % 2 + c) % 2)
            for i in range(nv)
            for j in range(nd)
        ]

    def swap_back(c):
        return [(b, a) for a, b in swap_route(c)]

    def in_order(got0, got1, axis):
        return jnp.concatenate(
            [jnp.where(odd, got1, got0), jnp.where(odd, got0, got1)], axis=axis
        )

    def turn(c):
        return [
            (
                (2 * a2 + b1) * nd + a * nb + 2 * core + x,
                (2 * a2 + core) * nd + a * nb + 2 * b1 + (x + c) % 2,
            )
            for a2 in range(na)
            for b1 in range(2)
            for a in range(na)
            for core in range(2)
            for x in range(2)
        ]

    def turn_back(c):
        return [(b, a) for a, b in turn(c)]

    def flip(x):
        return lax.ppermute(x, "core", [(0, 1), (1, 0)])

    weights = jnp.concatenate([proj_embed, proj_hidden], axis=0).T
    weights = gather(weights, "z", na)

    digits = jnp.stack([ids // 256, ids % 256]).astype(BF16)
    digits = in_order(
        lax.ppermute(digits, ALL, swap_route(0)), lax.ppermute(digits, ALL, swap_route(1)), 0
    )
    first, second = grad_out.T[:cw], grad_out.T[cw:]
    cot = in_order(
        lax.ppermute(jnp.where(odd, second, first), ALL, turn(0)),
        lax.ppermute(jnp.where(odd, first, second), ALL, turn(1)),
        0,
    )
    cot = jnp.concatenate([cot, jnp.pad(digits, ((0, 12), (0, 0)))], axis=0)
    cot, weights = lax.optimization_barrier((cot, weights))
    own = gather(cot, "chip", nc)
    other = flip(own)

    def ids_of(cot):
        digits = cot[:, fw : fw + 4].astype(jnp.int32)
        all_ids = 256 * digits[:, 0::2] + digits[:, 1::2]
        return (all_ids - v * entries).reshape(nc, 1, 2 * toks)

    own_ids, other_ids = ids_of(own), ids_of(other)

    shares = grad_products(place, weights, own, other, nb)
    grads = shares[0].astype(F32)
    for k in range(1, nb):
        grads += lax.ppermute(
            shares[k], "yhi", [(i, (i + k) % nb) for i in range(nb)]
        ).astype(F32)

    pieces = lookup(own_ids, table) + flip(lookup(other_ids, table))
    pieces = lax.all_to_all(pieces, "chip", 0, 0, tiled=True)
    cols = jnp.sum(pieces.astype(F32), axis=0).astype(BF16)
    first, second = cols[:, :toks], cols[:, toks:]
    embed = in_order(
        lax.ppermute(jnp.where(odd, second, first), ALL, swap_route(0)),
        lax.ppermute(jnp.where(odd, first, second), ALL, swap_route(1)),
        0,
    ).astype(F32)

    hid = hidden.T.astype(F32)
    gain_e, gain_h = gain_embed[:, None], gain_hidden[:, None]
    grad_left, grad_right = grads[:fw], grads[fw:]
    dn_embed, dn_hidden = grad_left * gain_e, grad_right * gain_h
    stats = jnp.stack(
        [
            jnp.sum(embed * embed, axis=0),
            jnp.sum(hid * hid, axis=0),
            jnp.sum(dn_embed * embed, axis=0),
            jnp.sum(dn_hidden * hid, axis=0),
        ]
    )
    stats = jnp.sum(gather(stats + flip(stats), "chip", nc), axis=0)
    inv_embed = lax.rsqrt(stats[0] / full + EPS)[None]
    inv_hidden = lax.rsqrt(stats[1] / full + EPS)[None]
    norm_embed, norm_hidden = embed * inv_embed, hid * inv_hidden
    coef_embed = stats[2][None] * inv_embed / full
    coef_hidden = stats[3][None] * inv_hidden / full
    grad_embedded = (inv_embed * (dn_embed - norm_embed * coef_embed)).astype(BF16)
    grad_hidden = (inv_hidden * (dn_hidden - norm_hidden * coef_hidden)).astype(BF16)

    gains = jnp.concatenate(
        [jnp.sum(grad_left * norm_embed, axis=1), jnp.sum(grad_right * norm_hidden, axis=1)]
    )
    lines = -(-2 * fw // toks)
    gains = jnp.pad(gains, (0, lines * toks - 2 * fw)).reshape(lines, toks)
    gains = jnp.pad(gains, ((0, 16 - lines), (0, 0)))
    gains_high = gains.astype(BF16)
    gains_low = (gains - gains_high.astype(F32)).astype(BF16)
    normed = gather(
        jnp.concatenate(
            [
                (norm_embed * gain_e).astype(BF16),
                (norm_hidden * gain_h).astype(BF16),
                gains_high,
                gains_low,
            ],
            axis=0,
        ),
        "yhi",
        nb,
    )

    low, high = grad_embedded[:cw], grad_embedded[cw:]
    mine = in_order(
        lax.ppermute(jnp.where(odd, high, low), ALL, swap_back(0)),
        lax.ppermute(jnp.where(odd, low, high), ALL, swap_back(1)),
        0,
    )

    normed, mine = lax.optimization_barrier((normed, mine))
    keep, send, weight_terms = out_products(place, weights, own, other, normed)
    terms = (keep.astype(F32) + flip(send).astype(F32)).astype(BF16)
    mine = jnp.broadcast_to(mine[None], (nc,) + mine.shape)
    both = lax.all_to_all(
        jnp.concatenate([terms, mine], axis=1), "chip", 0, 0, tiled=True
    )
    own_rows = both[:, fw:]
    grad_table, done = scatter(
        jnp.concatenate([own_ids, other_ids], axis=0), own_rows, flip(own_rows), entries
    )

    terms = jnp.sum(both[:, :fw].astype(F32), axis=0).astype(BF16)
    first, second = terms[:cw], terms[cw:]
    got0 = lax.ppermute(jnp.where(odd, second, first), ALL, turn_back(0))
    got1 = lax.ppermute(jnp.where(odd, first, second), ALL, turn_back(1))
    weight_terms = lax.psum_scatter(
        weight_terms.reshape(na * (cw + PAD_ROWS), 2 * fw), "z", scatter_dimension=0, tiled=True
    )
    projected, grad_embed, grad_hid, grad_gains = finish(
        place, weight_terms, got0, got1, done, lines
    )
    return (projected.T, grad_hidden.T, grad_table, grad_embed, grad_hid, grad_gains)


def solution(mesh):
    nv, nd = mesh.shape["vocab"], mesh.shape["dp"]
    nb = min(4, nd)
    split = Mesh(mesh.devices.reshape(nv // 2, 2, nd // nb, nb), ALL)
    rows = P(DP, VOCAB)
    return jax.shard_map(
        per_device,
        mesh=split,
        in_specs=(
            P(DP),
            rows,
            rows,
            P(VOCAB),
            P(VOCAB),
            P(VOCAB, DP),
            P(VOCAB, DP),
            rows,
        ),
        out_specs=(rows, rows, rows, P(VOCAB, DP), P(VOCAB, DP), P(None, VOCAB)),
        check_vma=False,
    )
```

```python
import functools

import jax
import jax.numpy as jnp
from jax import lax
from jax.experimental import pallas as pl
from jax.experimental.pallas import tpu as pltpu
from jax.sharding import Mesh
from jax.sharding import PartitionSpec as P

EPS = 1e-06
GROUPS = 8
PAD_ROWS = 80
BF16 = jnp.bfloat16
F32 = jnp.float32
DP = ("z", "yhi")
ALL = ("chip", "core", "z", "yhi")
VOCAB = ("chip", "core")


def gather(x, axes, count):
    return lax.all_to_all(
        jnp.broadcast_to(x[None], (count,) + x.shape), axes, 0, 0, tiled=True
    )


def one_hot_of(ids, width):
    rows = lax.broadcasted_iota(jnp.int32, (width, ids.shape[1]), 0)
    return jnp.where(rows == ids % width, 1.0, 0.0).astype(BF16)


def group_of(ids, width):
    return lax.div(jnp.where(ids < 0, -width, ids), width)


def lookup_kernel(ids_ref, table_ref, out_ref):
    parts, _, rows = ids_ref.shape
    width = table_ref.shape[1]
    cols = table_ref.shape[0] // GROUPS
    ids = jnp.concatenate([ids_ref[i] for i in range(parts)], axis=1)
    picked = jnp.dot(
        table_ref[...], one_hot_of(ids, width), preferred_element_type=F32
    )
    group = group_of(ids, width)
    total = jnp.zeros((cols, ids.shape[1]), F32)
    for k in range(GROUPS):
        total = jnp.where(group == k, picked[k * cols : (k + 1) * cols], total)
    for i in range(parts):
        out_ref[i] = total[:, i * rows : (i + 1) * rows].astype(BF16)


def stack_groups(table):
    cols, entries = table.shape
    width = entries // GROUPS
    return table.reshape(cols, GROUPS, width).transpose(1, 0, 2).reshape(cols * GROUPS, width)


def lookup(ids, stacked):
    blocks, _, rows = ids.shape
    width = stacked.shape[1]
    cols, entries = stacked.shape[0] // GROUPS, width * GROUPS
    parts = 4
    return pl.pallas_call(
        lookup_kernel,
        grid=(blocks // parts,),
        in_specs=[
            pl.BlockSpec((parts, 1, rows), lambda i: (i, 0, 0)),
            pl.BlockSpec((cols * GROUPS, width), lambda i: (0, 0)),
        ],
        out_specs=pl.BlockSpec((parts, cols, rows), lambda i: (i, 0, 0)),
        out_shape=jax.ShapeDtypeStruct((blocks, cols, rows), BF16),
        cost_estimate=pl.CostEstimate(
            flops=2 * blocks * rows * cols * entries,
            bytes_accessed=2 * cols * (entries + blocks * rows),
            transcendentals=0,
        ),
        compiler_params=pltpu.CompilerParams(vmem_limit_bytes=32 * 1024 * 1024),
    )(ids, stacked)


def scatter_kernel(ids_ref, own_ref, other_ref, out_ref, done_ref):
    width = out_ref.shape[1] // GROUPS
    cols = out_ref.shape[0]
    parts = ids_ref.shape[0]
    step = pl.program_id(0)
    own = 2 * step < pl.num_programs(0)
    ids = jnp.concatenate([ids_ref[i] for i in range(parts)], axis=1)
    values = jnp.concatenate(
        [
            jnp.where(
                own, own_ref[i, j * cols : (j + 1) * cols], other_ref[i, j * cols : (j + 1) * cols]
            )
            for i in range(parts)
            for j in range(2)
        ],
        axis=1,
    )
    group = group_of(ids, width)
    spread = jnp.concatenate(
        [values * jnp.where(group == k, 1.0, 0.0).astype(BF16) for k in range(GROUPS)], axis=0
    )
    sums = lax.dot_general(
        spread, one_hot_of(ids, width), (((1,), (1,)), ((), ())), preferred_element_type=F32
    )
    done_ref[...] = jnp.zeros_like(done_ref)

    @pl.when(pl.program_id(0) == 0)
    def _():
        for k in range(GROUPS):
            out_ref[:, k * width : (k + 1) * width] = sums[k * cols : (k + 1) * cols]

    @pl.when(pl.program_id(0) > 0)
    def _():
        for k in range(GROUPS):
            out_ref[:, k * width : (k + 1) * width] += sums[k * cols : (k + 1) * cols]


def scatter(ids, own, other, entries):
    blocks, rows, toks = own.shape
    cols = rows // 2
    parts = 4
    half = blocks // parts
    return pl.pallas_call(
        scatter_kernel,
        grid=(2 * half,),
        in_specs=[
            pl.BlockSpec((parts, 1, 2 * toks), lambda i: (i, 0, 0)),
            pl.BlockSpec((parts, 2 * cols, toks), lambda i: (jnp.minimum(i, half - 1), 0, 0)),
            pl.BlockSpec((parts, 2 * cols, toks), lambda i: (jnp.maximum(i - half, 0), 0, 0)),
        ],
        out_specs=(
            pl.BlockSpec((cols, entries), lambda i: (0, 0)),
            pl.BlockSpec((8, 128), lambda i: (0, 0)),
        ),
        out_shape=(
            jax.ShapeDtypeStruct((cols, entries), F32),
            jax.ShapeDtypeStruct((8, 128), F32),
        ),
        cost_estimate=pl.CostEstimate(
            flops=0,
            bytes_accessed=0,
            transcendentals=0,
        ),
        compiler_params=pltpu.CompilerParams(vmem_limit_bytes=32 * 1024 * 1024),
    )(ids, own, other)


def cot_columns(core, own_ref, other_ref, b, cw):
    half = b % 2 * cw
    own = core == b // 2
    return jnp.concatenate(
        [
            jnp.where(own, own_ref[i, half : half + cw], other_ref[i, half : half + cw])
            for i in range(own_ref.shape[0])
        ],
        axis=0,
    )


def grad_kernel(place_ref, weights_ref, own_ref, other_ref, keep_ref, send_ref):
    cw = weights_ref.shape[1]
    core, yhi = place_ref[0], place_ref[1]
    odd, far = lax.rem(yhi, 2), lax.div(yhi, 2)
    weights = jnp.concatenate([weights_ref[a] for a in range(weights_ref.shape[0])], axis=0).T
    for m in range(2):
        even_share, odd_share = (
            jnp.dot(
                weights, cot_columns(core, own_ref, other_ref, b, cw), preferred_element_type=F32
            )
            for b in (2 * m, 2 * m + 1)
        )
        slot = m + far - 2 * m * far
        keep_ref[slot] = jnp.where(odd == 1, odd_share, even_share).astype(BF16)
        send_ref[slot] = jnp.where(odd == 1, even_share, odd_share).astype(BF16)


def grad_products(place, weights, own, other):
    na, cw, feats = weights.shape
    toks = own.shape[2]
    whole = pl.BlockSpec(memory_space=pltpu.VMEM)
    return pl.pallas_call(
        grad_kernel,
        in_specs=[pl.BlockSpec(memory_space=pltpu.SMEM), whole, whole, whole],
        out_shape=(jax.ShapeDtypeStruct((2, feats, toks), BF16),) * 2,
        cost_estimate=pl.CostEstimate(
            flops=8 * na * cw * feats * toks,
            bytes_accessed=2 * (weights.size + 2 * own.size + 4 * feats * toks),
            transcendentals=0,
        ),
        compiler_params=pltpu.CompilerParams(vmem_limit_bytes=16 * 1024 * 1024),
    )(place, weights, own, other)


def out_kernel(
    place_ref, weights_ref, own_ref, other_ref, normed_ref, keep_ref, send_ref, sums_ref
):
    na, cw, feats = weights_ref.shape
    nb, _, toks = normed_ref.shape
    core = place_ref[0]
    weights = jnp.concatenate([weights_ref[a] for a in range(na)], axis=0)
    terms = [
        jnp.dot(weights, normed_ref[b, :feats], preferred_element_type=F32) for b in range(nb)
    ]
    for x in range(2):
        keep = jnp.where(core == 0, terms[x], terms[x + 2]).astype(BF16)
        send = jnp.where(core == 0, terms[x + 2], terms[x]).astype(BF16)
        for a in range(na):
            keep_ref[a, x * cw : (x + 1) * cw] = keep[a * cw : (a + 1) * cw]
            send_ref[a, x * cw : (x + 1) * cw] = send[a * cw : (a + 1) * cw]
    cot = jnp.concatenate(
        [cot_columns(core, own_ref, other_ref, b, cw) for b in range(nb)], axis=1
    )
    normed = jnp.concatenate([normed_ref[b, :feats] for b in range(nb)], axis=1)
    sums = lax.dot_general(
        cot, normed, (((1,), (1,)), ((), ())), preferred_element_type=F32
    ).astype(BF16)
    gains = jnp.zeros((16, toks), F32)
    for b in range(nb):
        gains += normed_ref[b, feats : feats + 16].astype(F32)
        gains += normed_ref[b, feats + 16 : feats + 32].astype(F32)
    for a in range(na):
        sums_ref[a, :cw] = sums[a * cw : (a + 1) * cw]
        sums_ref[a, cw:] = jnp.zeros((PAD_ROWS, feats), BF16)
        sums_ref[a, cw : cw + 16, :toks] = gains.astype(BF16)


def out_products(place, weights, own, other, normed):
    na, cw, feats = weights.shape
    nb, _, toks = normed.shape
    whole = pl.BlockSpec(memory_space=pltpu.VMEM)
    return pl.pallas_call(
        out_kernel,
        in_specs=[pl.BlockSpec(memory_space=pltpu.SMEM), whole, whole, whole, whole],
        out_shape=(
            jax.ShapeDtypeStruct((na, 2 * cw, toks), BF16),
            jax.ShapeDtypeStruct((na, 2 * cw, toks), BF16),
            jax.ShapeDtypeStruct((na, cw + PAD_ROWS, feats), BF16),
        ),
        cost_estimate=pl.CostEstimate(
            flops=4 * na * cw * feats * nb * toks,
            bytes_accessed=2 * (weights.size + 4 * own.size + normed.size + na * cw * feats),
            transcendentals=0,
        ),
        compiler_params=pltpu.CompilerParams(vmem_limit_bytes=32 * 1024 * 1024),
    )(place, weights, own, other, normed)


def finish_kernel(
    lines, place_ref, sums_ref, got0_ref, got1_ref, done_ref, out_ref, embed_ref, hidden_ref, gains_ref
):
    fw, cw = embed_ref.shape
    toks = out_ref.shape[1]
    odd = lax.rem(place_ref[1], 2) == 1
    out_ref[:cw] = jnp.where(odd, got1_ref[...], got0_ref[...])
    out_ref[cw:] = jnp.where(odd, got0_ref[...], got1_ref[...])
    sums = sums_ref[...].astype(F32)
    turned = sums[:cw].T
    embed_ref[...] = turned[:fw]
    hidden_ref[...] = turned[fw:]
    gains = jnp.concatenate(
        [sums[cw + i : cw + i + 1, :toks] for i in range(lines)], axis=1
    )
    gains_ref[0:1, :] = gains[:, :fw]
    gains_ref[1:2, :] = gains[:, fw : 2 * fw]


def finish(place, sums, got0, got1, done, lines):
    fw = sums.shape[1] // 2
    cw, toks = got0.shape
    whole = pl.BlockSpec(memory_space=pltpu.VMEM)
    return pl.pallas_call(
        functools.partial(finish_kernel, lines),
        in_specs=[pl.BlockSpec(memory_space=pltpu.SMEM), whole, whole, whole, whole],
        out_shape=(
            jax.ShapeDtypeStruct((2 * cw, toks), BF16),
            jax.ShapeDtypeStruct((fw, cw), F32),
            jax.ShapeDtypeStruct((fw, cw), F32),
            jax.ShapeDtypeStruct((2, fw), F32),
        ),
        cost_estimate=pl.CostEstimate(
            flops=0, bytes_accessed=2 * sums.size + 8 * fw * cw, transcendentals=0
        ),
    )(place, sums, got0, got1, done)


def per_device(ids, hidden, table, gain_embed, gain_hidden, proj_embed, proj_hidden, grad_out):
    core = lax.axis_index("core")
    v = 2 * lax.axis_index("chip") + core
    nc = lax.axis_size("chip")
    nv = 2 * nc
    na, nb = lax.axis_size("z"), lax.axis_size("yhi")
    nd = na * nb
    yhi = lax.axis_index("yhi")
    d = lax.axis_index("z") * nb + yhi
    place = jnp.stack([core, yhi]).astype(jnp.int32)
    odd = d % 2 == 1
    toks, fw = hidden.shape
    cw, entries = table.shape
    full = fw * nv

    def swap_route(c):
        return [
            (i * nd + j, (j // 2) * nd + 2 * i + (j % 2 + c) % 2)
            for i in range(nv)
            for j in range(nd)
        ]

    def swap_back(c):
        return [(b, a) for a, b in swap_route(c)]

    def in_order(got0, got1, axis):
        return jnp.concatenate(
            [jnp.where(odd, got1, got0), jnp.where(odd, got0, got1)], axis=axis
        )

    def turn(c):
        return [
            (
                (2 * a2 + b1) * nd + a * nb + 2 * core + x,
                (2 * a2 + core) * nd + a * nb + 2 * b1 + (x + c) % 2,
            )
            for a2 in range(na)
            for b1 in range(2)
            for a in range(na)
            for core in range(2)
            for x in range(2)
        ]

    def turn_back(c):
        return [(b, a) for a, b in turn(c)]

    def flip(x):
        return lax.ppermute(x, "core", [(0, 1), (1, 0)])

    weights = jnp.concatenate([proj_embed, proj_hidden], axis=0).T
    weights = gather(weights, "z", na)

    digits = jnp.stack([ids // 256, ids % 256]).astype(BF16)
    digits = in_order(
        lax.ppermute(digits, ALL, swap_route(0)), lax.ppermute(digits, ALL, swap_route(1)), 0
    )
    first, second = grad_out.T[:cw], grad_out.T[cw:]
    cot = in_order(
        lax.ppermute(jnp.where(odd, second, first), ALL, turn(0)),
        lax.ppermute(jnp.where(odd, first, second), ALL, turn(1)),
        0,
    )
    cot = jnp.concatenate([cot, jnp.pad(digits, ((0, 12), (0, 0)))], axis=0)
    cot, weights, stacked = lax.optimization_barrier((cot, weights, stack_groups(table)))
    own = gather(cot, "chip", nc)
    other = flip(own)

    def ids_of(cot):
        digits = cot[:, fw : fw + 4].astype(jnp.int32)
        all_ids = 256 * digits[:, 0::2] + digits[:, 1::2]
        return (all_ids - v * entries).reshape(nc, 1, 2 * toks)

    own_ids, other_ids = ids_of(own), ids_of(other)

    keep, send = grad_products(place, weights, own, other)
    pair = keep.astype(F32) + lax.ppermute(
        send, "yhi", [(i, i ^ 1) for i in range(nb)]
    ).astype(F32)
    grads = pair[0] + lax.ppermute(
        pair[1].astype(BF16), "yhi", [(i, i ^ 2) for i in range(nb)]
    ).astype(F32)

    pieces = lookup(own_ids, stacked) + flip(lookup(other_ids, stacked))
    pieces = lax.all_to_all(pieces, "chip", 0, 0, tiled=True)
    cols = jnp.sum(pieces.astype(F32), axis=0).astype(BF16)
    first, second = cols[:, :toks], cols[:, toks:]
    embed = in_order(
        lax.ppermute(jnp.where(odd, second, first), ALL, swap_route(0)),
        lax.ppermute(jnp.where(odd, first, second), ALL, swap_route(1)),
        0,
    ).astype(F32)

    hid = hidden.T.astype(F32)
    gain_e, gain_h = gain_embed[:, None], gain_hidden[:, None]
    grad_left, grad_right = grads[:fw], grads[fw:]
    dn_embed, dn_hidden = grad_left * gain_e, grad_right * gain_h
    stats = jnp.stack(
        [
            jnp.sum(embed * embed, axis=0),
            jnp.sum(hid * hid, axis=0),
            jnp.sum(dn_embed * embed, axis=0),
            jnp.sum(dn_hidden * hid, axis=0),
        ]
    )
    stats = jnp.sum(gather(stats + flip(stats), "chip", nc), axis=0)
    inv_embed = lax.rsqrt(stats[0] / full + EPS)[None]
    inv_hidden = lax.rsqrt(stats[1] / full + EPS)[None]
    norm_embed, norm_hidden = embed * inv_embed, hid * inv_hidden
    coef_embed = stats[2][None] * inv_embed / full
    coef_hidden = stats[3][None] * inv_hidden / full
    grad_embedded = (inv_embed * (dn_embed - norm_embed * coef_embed)).astype(BF16)
    grad_hidden = (inv_hidden * (dn_hidden - norm_hidden * coef_hidden)).astype(BF16)

    gains = jnp.concatenate(
        [jnp.sum(grad_left * norm_embed, axis=1), jnp.sum(grad_right * norm_hidden, axis=1)]
    )
    lines = -(-2 * fw // toks)
    gains = jnp.pad(gains, (0, lines * toks - 2 * fw)).reshape(lines, toks)
    gains = jnp.pad(gains, ((0, 16 - lines), (0, 0)))
    gains_high = gains.astype(BF16)
    gains_low = (gains - gains_high.astype(F32)).astype(BF16)
    normed = gather(
        jnp.concatenate(
            [
                (norm_embed * gain_e).astype(BF16),
                (norm_hidden * gain_h).astype(BF16),
                gains_high,
                gains_low,
            ],
            axis=0,
        ),
        "yhi",
        nb,
    )

    low, high = grad_embedded[:cw], grad_embedded[cw:]
    mine = in_order(
        lax.ppermute(jnp.where(odd, high, low), ALL, swap_back(0)),
        lax.ppermute(jnp.where(odd, low, high), ALL, swap_back(1)),
        0,
    )

    normed, mine = lax.optimization_barrier((normed, mine))
    keep, send, weight_terms = out_products(place, weights, own, other, normed)
    terms = (keep.astype(F32) + flip(send).astype(F32)).astype(BF16)
    mine = jnp.broadcast_to(mine[None], (nc,) + mine.shape)
    both = lax.all_to_all(
        jnp.concatenate([terms, mine], axis=1), "chip", 0, 0, tiled=True
    )
    own_rows = both[:, fw:]
    grad_table, done = scatter(
        jnp.concatenate([own_ids, other_ids], axis=0), own_rows, flip(own_rows), entries
    )

    terms = jnp.sum(both[:, :fw].astype(F32), axis=0).astype(BF16)
    first, second = terms[:cw], terms[cw:]
    got0 = lax.ppermute(jnp.where(odd, second, first), ALL, turn_back(0))
    got1 = lax.ppermute(jnp.where(odd, first, second), ALL, turn_back(1))
    weight_terms = lax.psum_scatter(
        weight_terms.reshape(na * (cw + PAD_ROWS), 2 * fw), "z", scatter_dimension=0, tiled=True
    )
    projected, grad_embed, grad_hid, grad_gains = finish(
        place, weight_terms, got0, got1, done, lines
    )
    return (projected.T, grad_hidden.T, grad_table, grad_embed, grad_hid, grad_gains)


def solution(mesh):
    nv, nd = mesh.shape["vocab"], mesh.shape["dp"]
    nb = min(4, nd)
    split = Mesh(mesh.devices.reshape(nv // 2, 2, nd // nb, nb), ALL)
    rows = P(DP, VOCAB)
    return jax.shard_map(
        per_device,
        mesh=split,
        in_specs=(
            P(DP),
            rows,
            rows,
            P(VOCAB),
            P(VOCAB),
            P(VOCAB, DP),
            P(VOCAB, DP),
            rows,
        ),
        out_specs=(rows, rows, rows, P(VOCAB, DP), P(VOCAB, DP), P(None, VOCAB)),
        check_vma=False,
    )
```

```python
import functools

import jax
import jax.numpy as jnp
from jax import lax
from jax.experimental import pallas as pl
from jax.experimental.pallas import tpu as pltpu
from jax.sharding import Mesh
from jax.sharding import PartitionSpec as P

EPS = 1e-06
GROUPS = 8
PAD_ROWS = 64
BF16 = jnp.bfloat16
F32 = jnp.float32
DP = ("z", "yhi")
ALL = ("chip", "core", "z", "yhi")
VOCAB = ("chip", "core")


def gather(x, axes, count):
    return lax.all_to_all(
        jnp.broadcast_to(x[None], (count,) + x.shape), axes, 0, 0, tiled=True
    )


def one_hot_of(ids, width):
    rows = lax.broadcasted_iota(jnp.int32, (width, ids.shape[1]), 0)
    return jnp.where(rows == ids % width, 1.0, 0.0).astype(BF16)


def group_of(ids, width):
    return lax.div(jnp.where(ids < 0, -width, ids), width)


def lookup_kernel(ids_ref, table_ref, out_ref):
    parts, _, rows = ids_ref.shape
    width = table_ref.shape[1]
    cols = table_ref.shape[0] // GROUPS
    ids = jnp.concatenate([ids_ref[i] for i in range(parts)], axis=1)
    picked = jnp.dot(
        table_ref[...], one_hot_of(ids, width), preferred_element_type=F32
    )
    group = group_of(ids, width)
    total = jnp.zeros((cols, ids.shape[1]), F32)
    for k in range(GROUPS):
        total = jnp.where(group == k, picked[k * cols : (k + 1) * cols], total)
    for i in range(parts):
        out_ref[i] = total[:, i * rows : (i + 1) * rows].astype(BF16)


def lookup(ids, table):
    blocks, _, rows = ids.shape
    cols, entries = table.shape
    width = entries // GROUPS
    parts = 4
    stacked = table.reshape(cols, GROUPS, width).transpose(1, 0, 2).reshape(cols * GROUPS, width)
    return pl.pallas_call(
        lookup_kernel,
        grid=(blocks // parts,),
        in_specs=[
            pl.BlockSpec((parts, 1, rows), lambda i: (i, 0, 0)),
            pl.BlockSpec((cols * GROUPS, width), lambda i: (0, 0)),
        ],
        out_specs=pl.BlockSpec((parts, cols, rows), lambda i: (i, 0, 0)),
        out_shape=jax.ShapeDtypeStruct((blocks, cols, rows), BF16),
        cost_estimate=pl.CostEstimate(
            flops=2 * blocks * rows * cols * entries,
            bytes_accessed=2 * cols * (entries + blocks * rows),
            transcendentals=0,
        ),
        compiler_params=pltpu.CompilerParams(vmem_limit_bytes=32 * 1024 * 1024),
    )(ids, stacked)


def scatter_kernel(ids_ref, own_ref, other_ref, out_ref, done_ref):
    width = out_ref.shape[1] // GROUPS
    cols = out_ref.shape[0]
    parts = ids_ref.shape[0]
    step = pl.program_id(0)
    own = 2 * step < pl.num_programs(0)
    ids = jnp.concatenate([ids_ref[i] for i in range(parts)], axis=1)
    values = jnp.concatenate(
        [
            jnp.where(
                own, own_ref[i, j * cols : (j + 1) * cols], other_ref[i, j * cols : (j + 1) * cols]
            )
            for i in range(parts)
            for j in range(2)
        ],
        axis=1,
    )
    group = group_of(ids, width)
    spread = jnp.concatenate(
        [values * jnp.where(group == k, 1.0, 0.0).astype(BF16) for k in range(GROUPS)], axis=0
    )
    sums = lax.dot_general(
        spread, one_hot_of(ids, width), (((1,), (1,)), ((), ())), preferred_element_type=F32
    )
    done_ref[...] = jnp.zeros_like(done_ref)

    @pl.when(pl.program_id(0) == 0)
    def _():
        for k in range(GROUPS):
            out_ref[:, k * width : (k + 1) * width] = sums[k * cols : (k + 1) * cols]

    @pl.when(pl.program_id(0) > 0)
    def _():
        for k in range(GROUPS):
            out_ref[:, k * width : (k + 1) * width] += sums[k * cols : (k + 1) * cols]


def scatter(ids, own, other, entries):
    blocks, rows, toks = own.shape
    cols = rows // 2
    parts = 4
    half = blocks // parts
    return pl.pallas_call(
        scatter_kernel,
        grid=(2 * half,),
        in_specs=[
            pl.BlockSpec((parts, 1, 2 * toks), lambda i: (i, 0, 0)),
            pl.BlockSpec((parts, 2 * cols, toks), lambda i: (jnp.minimum(i, half - 1), 0, 0)),
            pl.BlockSpec((parts, 2 * cols, toks), lambda i: (jnp.maximum(i - half, 0), 0, 0)),
        ],
        out_specs=(
            pl.BlockSpec((cols, entries), lambda i: (0, 0)),
            pl.BlockSpec((8, 128), lambda i: (0, 0)),
        ),
        out_shape=(
            jax.ShapeDtypeStruct((cols, entries), F32),
            jax.ShapeDtypeStruct((8, 128), F32),
        ),
        cost_estimate=pl.CostEstimate(
            flops=0,
            bytes_accessed=0,
            transcendentals=0,
        ),
        compiler_params=pltpu.CompilerParams(vmem_limit_bytes=32 * 1024 * 1024),
    )(ids, own, other)


def cot_columns(core, own_ref, other_ref, b, cw):
    half = b % 2 * cw
    own = core == b // 2
    return jnp.concatenate(
        [
            jnp.where(own, own_ref[i, half : half + cw], other_ref[i, half : half + cw])
            for i in range(own_ref.shape[0])
        ],
        axis=0,
    )


def grad_kernel(cw, place_ref, weights_ref, own_ref, other_ref, out_ref):
    nb, feats, _ = out_ref.shape
    weights = jnp.concatenate([weights_ref[a] for a in range(weights_ref.shape[0])], axis=0).T
    whole = [
        jnp.dot(
            weights,
            cot_columns(place_ref[0], own_ref, other_ref, b, cw),
            preferred_element_type=F32,
        ).astype(BF16)
        for b in range(nb)
    ]
    for b in range(nb):
        half, pair = b % 2 * cw, b // 2 * 2
        share = [whole[pair + x][half : half + cw] for x in range(2)] + [whole[b][2 * cw :]]
        out_ref[lax.rem(b + nb - place_ref[1], nb)] = jnp.concatenate(share, axis=0)


def grad_products(place, weights, own, other, nb):
    na, cw, feats = weights.shape
    toks = own.shape[2]
    whole = pl.BlockSpec(memory_space=pltpu.VMEM)
    return pl.pallas_call(
        functools.partial(grad_kernel, cw),
        in_specs=[pl.BlockSpec(memory_space=pltpu.SMEM), whole, whole, whole],
        out_shape=jax.ShapeDtypeStruct((nb, feats, toks), BF16),
        cost_estimate=pl.CostEstimate(
            flops=2 * na * cw * feats * nb * toks,
            bytes_accessed=2 * (weights.size + 2 * own.size + nb * feats * toks),
            transcendentals=0,
        ),
        compiler_params=pltpu.CompilerParams(vmem_limit_bytes=16 * 1024 * 1024),
    )(place, weights, own, other)


def normed_columns(normed_ref, b, cw):
    pair, x = b // 2 * 2, b % 2 * cw
    return jnp.concatenate(
        [normed_ref[pair, x : x + cw], normed_ref[pair + 1, x : x + cw], normed_ref[b, 2 * cw : 4 * cw]],
        axis=0,
    )


def out_kernel(
    place_ref, weights_ref, own_ref, other_ref, normed_ref, keep_ref, send_ref, sums_ref
):
    na, cw, feats = weights_ref.shape
    nb, _, toks = normed_ref.shape
    core = place_ref[0]
    weights = jnp.concatenate([weights_ref[a] for a in range(na)], axis=0)
    blocks = [normed_columns(normed_ref, b, cw) for b in range(nb)]
    terms = [jnp.dot(weights, block, preferred_element_type=F32) for block in blocks]
    for x in range(2):
        keep = jnp.where(core == 0, terms[x], terms[x + 2]).astype(BF16)
        send = jnp.where(core == 0, terms[x + 2], terms[x]).astype(BF16)
        for a in range(na):
            keep_ref[a, x * cw : (x + 1) * cw] = keep[a * cw : (a + 1) * cw]
            send_ref[a, x * cw : (x + 1) * cw] = send[a * cw : (a + 1) * cw]
    cot = jnp.concatenate(
        [cot_columns(core, own_ref, other_ref, b, cw) for b in range(nb)], axis=1
    )
    normed = jnp.concatenate(blocks, axis=1)
    sums = lax.dot_general(
        cot, normed, (((1,), (1,)), ((), ())), preferred_element_type=F32
    ).astype(BF16)
    gains = jnp.zeros((16, toks), F32)
    for b in range(nb):
        gains += normed_ref[b, feats : feats + 16].astype(F32)
        gains += normed_ref[b, feats + 16 : feats + 32].astype(F32)
    for a in range(na):
        sums_ref[a, :cw] = sums[a * cw : (a + 1) * cw]
        sums_ref[a, cw:] = jnp.zeros((PAD_ROWS, feats), BF16)
        sums_ref[a, cw : cw + 16, :toks] = gains.astype(BF16)


def out_products(place, weights, own, other, normed):
    na, cw, feats = weights.shape
    nb, _, toks = normed.shape
    whole = pl.BlockSpec(memory_space=pltpu.VMEM)
    return pl.pallas_call(
        out_kernel,
        in_specs=[pl.BlockSpec(memory_space=pltpu.SMEM), whole, whole, whole, whole],
        out_shape=(
            jax.ShapeDtypeStruct((na, 2 * cw, toks), BF16),
            jax.ShapeDtypeStruct((na, 2 * cw, toks), BF16),
            jax.ShapeDtypeStruct((na, cw + PAD_ROWS, feats), BF16),
        ),
        cost_estimate=pl.CostEstimate(
            flops=4 * na * cw * feats * nb * toks,
            bytes_accessed=2 * (weights.size + 4 * own.size + normed.size + na * cw * feats),
            transcendentals=0,
        ),
        compiler_params=pltpu.CompilerParams(vmem_limit_bytes=32 * 1024 * 1024),
    )(place, weights, own, other, normed)


def finish_kernel(
    lines, place_ref, sums_ref, got0_ref, got1_ref, done_ref, out_ref, embed_ref, hidden_ref, gains_ref
):
    fw, cw = embed_ref.shape
    toks = out_ref.shape[1]
    odd = lax.rem(place_ref[1], 2) == 1
    out_ref[:cw] = jnp.where(odd, got1_ref[...], got0_ref[...])
    out_ref[cw:] = jnp.where(odd, got0_ref[...], got1_ref[...])
    sums = sums_ref[...].astype(F32)
    turned = sums[:cw].T
    embed_ref[...] = turned[:fw]
    hidden_ref[...] = turned[fw:]
    gains = jnp.concatenate(
        [sums[cw + i : cw + i + 1, :toks] for i in range(lines)], axis=1
    )
    gains_ref[0:1, :] = gains[:, :fw]
    gains_ref[1:2, :] = gains[:, fw : 2 * fw]


def finish(place, sums, got0, got1, done, lines):
    fw = sums.shape[1] // 2
    cw, toks = got0.shape
    whole = pl.BlockSpec(memory_space=pltpu.VMEM)
    return pl.pallas_call(
        functools.partial(finish_kernel, lines),
        in_specs=[pl.BlockSpec(memory_space=pltpu.SMEM), whole, whole, whole, whole],
        out_shape=(
            jax.ShapeDtypeStruct((2 * cw, toks), BF16),
            jax.ShapeDtypeStruct((fw, cw), F32),
            jax.ShapeDtypeStruct((fw, cw), F32),
            jax.ShapeDtypeStruct((2, fw), F32),
        ),
        cost_estimate=pl.CostEstimate(
            flops=0, bytes_accessed=0, transcendentals=0
        ),
    )(place, sums, got0, got1, done)


def per_device(ids, hidden, table, gain_embed, gain_hidden, proj_embed, proj_hidden, grad_out):
    core = lax.axis_index("core")
    v = 2 * lax.axis_index("chip") + core
    nc = lax.axis_size("chip")
    nv = 2 * nc
    na, nb = lax.axis_size("z"), lax.axis_size("yhi")
    nd = na * nb
    yhi = lax.axis_index("yhi")
    d = lax.axis_index("z") * nb + yhi
    place = jnp.stack([core, yhi]).astype(jnp.int32)
    odd = d % 2 == 1
    toks, fw = hidden.shape
    cw, entries = table.shape
    full = fw * nv

    def swap_route(c):
        return [
            (i * nd + j, (j // 2) * nd + 2 * i + (j % 2 + c) % 2)
            for i in range(nv)
            for j in range(nd)
        ]

    across = [
        ((2 * p + c) * nd + q * nb + 2 * c2 + i, (2 * q + c2) * nd + p * nb + 2 * c + i)
        for p in range(na)
        for c in range(2)
        for q in range(na)
        for c2 in range(2)
        for i in range(2)
    ]

    def in_order(got0, got1, axis):
        return jnp.concatenate(
            [jnp.where(odd, got1, got0), jnp.where(odd, got0, got1)], axis=axis
        )

    def turn(c):
        return [
            (
                (2 * a2 + b1) * nd + a * nb + 2 * core + x,
                (2 * a2 + core) * nd + a * nb + 2 * b1 + (x + c) % 2,
            )
            for a2 in range(na)
            for b1 in range(2)
            for a in range(na)
            for core in range(2)
            for x in range(2)
        ]

    def turn_back(c):
        return [(b, a) for a, b in turn(c)]

    def flip(x):
        return lax.ppermute(x, "core", [(0, 1), (1, 0)])

    weights = jnp.concatenate([proj_embed, proj_hidden], axis=0).T
    weights = gather(weights, "z", na)

    digits = jnp.stack([ids // 256, ids % 256]).astype(BF16)
    digits = in_order(
        lax.ppermute(digits, ALL, swap_route(0)), lax.ppermute(digits, ALL, swap_route(1)), 0
    )
    first, second = grad_out.T[:cw], grad_out.T[cw:]
    cot = in_order(
        lax.ppermute(jnp.where(odd, second, first), ALL, turn(0)),
        lax.ppermute(jnp.where(odd, first, second), ALL, turn(1)),
        0,
    )
    cot = jnp.concatenate([cot, jnp.pad(digits, ((0, 12), (0, 0)))], axis=0)
    cot, weights = lax.optimization_barrier((cot, weights))
    own = gather(cot, "chip", nc)
    other = flip(own)

    def ids_of(cot):
        digits = cot[:, fw : fw + 4].astype(jnp.int32)
        all_ids = 256 * digits[:, 0::2] + digits[:, 1::2]
        return (all_ids - v * entries).reshape(nc, 1, 2 * toks)

    own_ids, other_ids = ids_of(own), ids_of(other)

    shares = grad_products(place, weights, own, other, nb)
    grads = shares[0].astype(F32)
    for k in range(1, nb):
        grads += lax.ppermute(
            shares[k], "yhi", [(i, (i + k) % nb) for i in range(nb)]
        ).astype(F32)

    pieces = lookup(own_ids, table) + flip(lookup(other_ids, table))
    pieces = lax.all_to_all(pieces, "chip", 0, 0, tiled=True)
    cols = jnp.sum(pieces.astype(F32), axis=0).astype(BF16)
    embed = jnp.concatenate([cols[:, :toks], cols[:, toks:]], axis=0)
    embed = lax.ppermute(embed, ALL, across).astype(F32)

    def by_block(x):
        return jnp.sum(x.reshape(2, cw, toks), axis=1)

    def to_rows(x):
        return jnp.broadcast_to(x[:, None], (2, cw, toks)).reshape(2 * cw, toks)

    hid = hidden.T.astype(F32)
    gain_e = jnp.where(odd, gain_embed[cw:], gain_embed[:cw])
    gain_e, gain_h = jnp.concatenate([gain_e, gain_e])[:, None], gain_hidden[:, None]
    grad_left, grad_right = grads[:fw], grads[fw:]
    dn_embed, dn_hidden = grad_left * gain_e, grad_right * gain_h
    halves = jnp.concatenate([by_block(embed * embed), by_block(dn_embed * embed)], axis=0)
    halves += lax.ppermute(halves, "yhi", [(i, i ^ 1) for i in range(nb)])
    stats = jnp.concatenate(
        [
            halves,
            jnp.sum(hid * hid, axis=0, keepdims=True),
            jnp.sum(dn_hidden * hid, axis=0, keepdims=True),
        ],
        axis=0,
    )
    stats = jnp.sum(gather(stats, VOCAB, nv), axis=0)
    inv_embed = lax.rsqrt(stats[:2] / full + EPS)
    coef_embed = to_rows(stats[2:4] * inv_embed / full)
    inv_embed = to_rows(inv_embed)
    inv_hidden = lax.rsqrt(stats[4:5] / full + EPS)
    coef_hidden = stats[5:6] * inv_hidden / full
    norm_embed, norm_hidden = embed * inv_embed, hid * inv_hidden
    grad_embedded = (inv_embed * (dn_embed - norm_embed * coef_embed)).astype(BF16)
    grad_hidden = (inv_hidden * (dn_hidden - norm_hidden * coef_hidden)).astype(BF16)

    gains = jnp.sum(grad_left * norm_embed, axis=1)
    gains = gains[:cw] + gains[cw:]
    gains = jnp.concatenate(
        [
            jnp.where(odd, 0.0, gains),
            jnp.where(odd, gains, 0.0),
            jnp.sum(grad_right * norm_hidden, axis=1),
        ]
    )
    lines = -(-2 * fw // toks)
    gains = jnp.pad(gains, (0, lines * toks - 2 * fw)).reshape(lines, toks)
    gains = jnp.pad(gains, ((0, 16 - lines), (0, 0)))
    gains_high = gains.astype(BF16)
    gains_low = (gains - gains_high.astype(F32)).astype(BF16)
    normed = gather(
        jnp.concatenate(
            [
                (norm_embed * gain_e).astype(BF16),
                (norm_hidden * gain_h).astype(BF16),
                gains_high,
                gains_low,
            ],
            axis=0,
        ),
        "yhi",
        nb,
    )

    mine = lax.ppermute(grad_embedded, ALL, across)

    normed, mine = lax.optimization_barrier((normed, mine))
    keep, send, weight_terms = out_products(place, weights, own, other, normed)
    terms = (keep.astype(F32) + flip(send).astype(F32)).astype(BF16)
    mine = jnp.broadcast_to(mine[None], (nc,) + mine.shape)
    both = lax.all_to_all(
        jnp.concatenate([terms, mine], axis=1), "chip", 0, 0, tiled=True
    )
    own_rows = both[:, fw:]
    grad_table, done = scatter(
        jnp.concatenate([own_ids, other_ids], axis=0), own_rows, flip(own_rows), entries
    )

    terms = jnp.sum(both[:, :fw].astype(F32), axis=0).astype(BF16)
    first, second = terms[:cw], terms[cw:]
    got0 = lax.ppermute(jnp.where(odd, second, first), ALL, turn_back(0))
    got1 = lax.ppermute(jnp.where(odd, first, second), ALL, turn_back(1))
    weight_terms = lax.psum_scatter(
        weight_terms.reshape(na * (cw + PAD_ROWS), 2 * fw), "z", scatter_dimension=0, tiled=True
    )
    projected, grad_embed, grad_hid, grad_gains = finish(
        place, weight_terms, got0, got1, done, lines
    )
    return (projected.T, grad_hidden.T, grad_table, grad_embed, grad_hid, grad_gains)


def solution(mesh):
    nv, nd = mesh.shape["vocab"], mesh.shape["dp"]
    nb = min(4, nd)
    split = Mesh(mesh.devices.reshape(nv // 2, 2, nd // nb, nb), ALL)
    rows = P(DP, VOCAB)
    return jax.shard_map(
        per_device,
        mesh=split,
        in_specs=(
            P(DP),
            rows,
            rows,
            P(VOCAB),
            P(VOCAB),
            P(VOCAB, DP),
            P(VOCAB, DP),
            rows,
        ),
        out_specs=(rows, rows, rows, P(VOCAB, DP), P(VOCAB, DP), P(None, VOCAB)),
        check_vma=False,
    )
```

```python
import functools

import jax
import jax.numpy as jnp
from jax import lax
from jax.experimental import pallas as pl
from jax.experimental.pallas import tpu as pltpu
from jax.sharding import Mesh
from jax.sharding import PartitionSpec as P

EPS = 1e-06
GROUPS = 8
PAD_ROWS = 64
BF16 = jnp.bfloat16
F32 = jnp.float32
DP = ("z", "yhi")
ALL = ("chip", "core", "z", "yhi")
VOCAB = ("chip", "core")


def gather(x, axes, count):
    return lax.all_to_all(
        jnp.broadcast_to(x[None], (count,) + x.shape), axes, 0, 0, tiled=True
    )


def one_hot_of(ids, width):
    rows = lax.broadcasted_iota(jnp.int32, (width, ids.shape[1]), 0)
    return jnp.where(rows == ids % width, 1.0, 0.0).astype(BF16)


def group_of(ids, width):
    return lax.div(jnp.where(ids < 0, -width, ids), width)


def lookup_kernel(ids_ref, table_ref, out_ref):
    parts, _, rows = ids_ref.shape
    width = table_ref.shape[1]
    cols = table_ref.shape[0] // GROUPS
    ids = jnp.concatenate([ids_ref[i] for i in range(parts)], axis=1)
    picked = jnp.dot(
        table_ref[...], one_hot_of(ids, width), preferred_element_type=F32
    )
    group = group_of(ids, width)
    total = jnp.zeros((cols, ids.shape[1]), F32)
    for k in range(GROUPS):
        total = jnp.where(group == k, picked[k * cols : (k + 1) * cols], total)
    for i in range(parts):
        out_ref[i] = total[:, i * rows : (i + 1) * rows].astype(BF16)


def lookup(ids, table):
    blocks, _, rows = ids.shape
    cols, entries = table.shape
    width = entries // GROUPS
    parts = 4
    stacked = table.reshape(cols, GROUPS, width).transpose(1, 0, 2).reshape(cols * GROUPS, width)
    return pl.pallas_call(
        lookup_kernel,
        grid=(blocks // parts,),
        in_specs=[
            pl.BlockSpec((parts, 1, rows), lambda i: (i, 0, 0)),
            pl.BlockSpec((cols * GROUPS, width), lambda i: (0, 0)),
        ],
        out_specs=pl.BlockSpec((parts, cols, rows), lambda i: (i, 0, 0)),
        out_shape=jax.ShapeDtypeStruct((blocks, cols, rows), BF16),
        cost_estimate=pl.CostEstimate(
            flops=2 * blocks * rows * cols * entries,
            bytes_accessed=2 * cols * (entries + blocks * rows),
            transcendentals=0,
        ),
        compiler_params=pltpu.CompilerParams(vmem_limit_bytes=32 * 1024 * 1024),
    )(ids, stacked)


def scatter_kernel(ids_ref, own_ref, other_ref, out_ref, done_ref):
    width = out_ref.shape[1] // GROUPS
    cols = out_ref.shape[0]
    parts = ids_ref.shape[0]
    step = pl.program_id(0)
    own = 2 * step < pl.num_programs(0)
    ids = jnp.concatenate([ids_ref[i] for i in range(parts)], axis=1)
    values = jnp.concatenate(
        [
            jnp.where(
                own, own_ref[i, j * cols : (j + 1) * cols], other_ref[i, j * cols : (j + 1) * cols]
            )
            for i in range(parts)
            for j in range(2)
        ],
        axis=1,
    )
    group = group_of(ids, width)
    spread = jnp.concatenate(
        [values * jnp.where(group == k, 1.0, 0.0).astype(BF16) for k in range(GROUPS)], axis=0
    )
    sums = lax.dot_general(
        spread, one_hot_of(ids, width), (((1,), (1,)), ((), ())), preferred_element_type=F32
    )
    done_ref[...] = jnp.zeros_like(done_ref)

    @pl.when(pl.program_id(0) == 0)
    def _():
        for k in range(GROUPS):
            out_ref[:, k * width : (k + 1) * width] = sums[k * cols : (k + 1) * cols]

    @pl.when(pl.program_id(0) > 0)
    def _():
        for k in range(GROUPS):
            out_ref[:, k * width : (k + 1) * width] += sums[k * cols : (k + 1) * cols]


def scatter(ids, own, other, entries):
    blocks, rows, toks = own.shape
    cols = rows // 2
    parts = blocks
    half = blocks // parts
    return pl.pallas_call(
        scatter_kernel,
        grid=(2 * half,),
        in_specs=[
            pl.BlockSpec((parts, 1, 2 * toks), lambda i: (i, 0, 0)),
            pl.BlockSpec((parts, 2 * cols, toks), lambda i: (jnp.minimum(i, half - 1), 0, 0)),
            pl.BlockSpec((parts, 2 * cols, toks), lambda i: (jnp.maximum(i - half, 0), 0, 0)),
        ],
        out_specs=(
            pl.BlockSpec((cols, entries), lambda i: (0, 0)),
            pl.BlockSpec((8, 128), lambda i: (0, 0)),
        ),
        out_shape=(
            jax.ShapeDtypeStruct((cols, entries), F32),
            jax.ShapeDtypeStruct((8, 128), F32),
        ),
        cost_estimate=pl.CostEstimate(
            flops=0,
            bytes_accessed=0,
            transcendentals=0,
        ),
        compiler_params=pltpu.CompilerParams(vmem_limit_bytes=32 * 1024 * 1024),
    )(ids, own, other)


def cot_columns(core, own_ref, other_ref, b, cw):
    half = b % 2 * cw
    own = core == b // 2
    return jnp.concatenate(
        [
            jnp.where(own, own_ref[i, half : half + cw], other_ref[i, half : half + cw])
            for i in range(own_ref.shape[0])
        ],
        axis=0,
    )


def grad_kernel(cw, place_ref, weights_ref, own_ref, other_ref, out_ref):
    nb, feats, _ = out_ref.shape
    weights = jnp.concatenate([weights_ref[a] for a in range(weights_ref.shape[0])], axis=0).T
    whole = [
        jnp.dot(
            weights,
            cot_columns(place_ref[0], own_ref, other_ref, b, cw),
            preferred_element_type=F32,
        ).astype(BF16)
        for b in range(nb)
    ]
    for b in range(nb):
        half, pair = b % 2 * cw, b // 2 * 2
        share = [whole[pair + x][half : half + cw] for x in range(2)] + [whole[b][2 * cw :]]
        out_ref[b] = jnp.concatenate(share, axis=0)


def grad_products(place, weights, own, other, nb):
    na, cw, feats = weights.shape
    toks = own.shape[2]
    whole = pl.BlockSpec(memory_space=pltpu.VMEM)
    return pl.pallas_call(
        functools.partial(grad_kernel, cw),
        in_specs=[pl.BlockSpec(memory_space=pltpu.SMEM), whole, whole, whole],
        out_shape=jax.ShapeDtypeStruct((nb, feats, toks), BF16),
        cost_estimate=pl.CostEstimate(
            flops=2 * na * cw * feats * nb * toks,
            bytes_accessed=2 * (weights.size + 2 * own.size + nb * feats * toks),
            transcendentals=0,
        ),
        compiler_params=pltpu.CompilerParams(vmem_limit_bytes=16 * 1024 * 1024),
    )(place, weights, own, other)


def normed_columns(normed_ref, b, cw):
    pair, x = b // 2 * 2, b % 2 * cw
    return jnp.concatenate(
        [normed_ref[pair, x : x + cw], normed_ref[pair + 1, x : x + cw], normed_ref[b, 2 * cw : 4 * cw]],
        axis=0,
    )


def out_kernel(
    place_ref, weights_ref, own_ref, other_ref, normed_ref, keep_ref, send_ref, sums_ref
):
    na, cw, feats = weights_ref.shape
    nb, _, toks = normed_ref.shape
    core = place_ref[0]
    weights = jnp.concatenate([weights_ref[a] for a in range(na)], axis=0)
    blocks = [normed_columns(normed_ref, b, cw) for b in range(nb)]
    terms = [jnp.dot(weights, block, preferred_element_type=F32) for block in blocks]
    for x in range(2):
        keep = jnp.where(core == 0, terms[x], terms[x + 2]).astype(BF16)
        send = jnp.where(core == 0, terms[x + 2], terms[x]).astype(BF16)
        for a in range(na):
            keep_ref[a, x * cw : (x + 1) * cw] = keep[a * cw : (a + 1) * cw]
            send_ref[a, x * cw : (x + 1) * cw] = send[a * cw : (a + 1) * cw]
    cot = jnp.concatenate(
        [cot_columns(core, own_ref, other_ref, b, cw) for b in range(nb)], axis=1
    )
    normed = jnp.concatenate(blocks, axis=1)
    sums = lax.dot_general(
        cot, normed, (((1,), (1,)), ((), ())), preferred_element_type=F32
    ).astype(BF16)
    gains = jnp.zeros((16, toks), F32)
    for b in range(nb):
        gains += normed_ref[b, feats : feats + 16].astype(F32)
        gains += normed_ref[b, feats + 16 : feats + 32].astype(F32)
    for a in range(na):
        sums_ref[a, :cw] = sums[a * cw : (a + 1) * cw]
        sums_ref[a, cw:] = jnp.zeros((PAD_ROWS, feats), BF16)
        sums_ref[a, cw : cw + 16, :toks] = gains.astype(BF16)


def out_products(place, weights, own, other, normed):
    na, cw, feats = weights.shape
    nb, _, toks = normed.shape
    whole = pl.BlockSpec(memory_space=pltpu.VMEM)
    return pl.pallas_call(
        out_kernel,
        in_specs=[pl.BlockSpec(memory_space=pltpu.SMEM), whole, whole, whole, whole],
        out_shape=(
            jax.ShapeDtypeStruct((na, 2 * cw, toks), BF16),
            jax.ShapeDtypeStruct((na, 2 * cw, toks), BF16),
            jax.ShapeDtypeStruct((na, cw + PAD_ROWS, feats), BF16),
        ),
        cost_estimate=pl.CostEstimate(
            flops=4 * na * cw * feats * nb * toks,
            bytes_accessed=2 * (weights.size + 4 * own.size + normed.size + na * cw * feats),
            transcendentals=0,
        ),
        compiler_params=pltpu.CompilerParams(vmem_limit_bytes=32 * 1024 * 1024),
    )(place, weights, own, other, normed)


def finish_kernel(
    lines, place_ref, sums_ref, got0_ref, got1_ref, done_ref, out_ref, embed_ref, hidden_ref, gains_ref
):
    fw, cw = embed_ref.shape
    toks = out_ref.shape[1]
    odd = lax.rem(place_ref[1], 2) == 1
    out_ref[:cw] = jnp.where(odd, got1_ref[...], got0_ref[...])
    out_ref[cw:] = jnp.where(odd, got0_ref[...], got1_ref[...])
    sums = sums_ref[...].astype(F32)
    turned = sums[:cw].T
    embed_ref[...] = turned[:fw]
    hidden_ref[...] = turned[fw:]
    gains = jnp.concatenate(
        [sums[cw + i : cw + i + 1, :toks] for i in range(lines)], axis=1
    )
    gains_ref[0:1, :] = gains[:, :fw]
    gains_ref[1:2, :] = gains[:, fw : 2 * fw]


def finish(place, sums, got0, got1, done, lines):
    fw = sums.shape[1] // 2
    cw, toks = got0.shape
    whole = pl.BlockSpec(memory_space=pltpu.VMEM)
    return pl.pallas_call(
        functools.partial(finish_kernel, lines),
        in_specs=[pl.BlockSpec(memory_space=pltpu.SMEM), whole, whole, whole, whole],
        out_shape=(
            jax.ShapeDtypeStruct((2 * cw, toks), BF16),
            jax.ShapeDtypeStruct((fw, cw), F32),
            jax.ShapeDtypeStruct((fw, cw), F32),
            jax.ShapeDtypeStruct((2, fw), F32),
        ),
        cost_estimate=pl.CostEstimate(
            flops=0, bytes_accessed=0, transcendentals=0
        ),
    )(place, sums, got0, got1, done)


def per_device(ids, hidden, table, gain_embed, gain_hidden, proj_embed, proj_hidden, grad_out):
    core = lax.axis_index("core")
    v = 2 * lax.axis_index("chip") + core
    nc = lax.axis_size("chip")
    nv = 2 * nc
    na, nb = lax.axis_size("z"), lax.axis_size("yhi")
    nd = na * nb
    yhi = lax.axis_index("yhi")
    d = lax.axis_index("z") * nb + yhi
    place = jnp.stack([core, yhi]).astype(jnp.int32)
    odd = d % 2 == 1
    toks, fw = hidden.shape
    cw, entries = table.shape
    full = fw * nv

    def swap_route(c):
        return [
            (i * nd + j, (j // 2) * nd + 2 * i + (j % 2 + c) % 2)
            for i in range(nv)
            for j in range(nd)
        ]

    across = [
        ((2 * p + c) * nd + q * nb + 2 * c2 + i, (2 * q + c2) * nd + p * nb + 2 * c + i)
        for p in range(na)
        for c in range(2)
        for q in range(na)
        for c2 in range(2)
        for i in range(2)
    ]

    def in_order(got0, got1, axis):
        return jnp.concatenate(
            [jnp.where(odd, got1, got0), jnp.where(odd, got0, got1)], axis=axis
        )

    def turn(c):
        return [
            (
                (2 * a2 + b1) * nd + a * nb + 2 * core + x,
                (2 * a2 + core) * nd + a * nb + 2 * b1 + (x + c) % 2,
            )
            for a2 in range(na)
            for b1 in range(2)
            for a in range(na)
            for core in range(2)
            for x in range(2)
        ]

    def turn_back(c):
        return [(b, a) for a, b in turn(c)]

    def flip(x):
        return lax.ppermute(x, "core", [(0, 1), (1, 0)])

    weights = jnp.concatenate([proj_embed, proj_hidden], axis=0).T
    weights = gather(weights, "z", na)

    digits = jnp.stack([ids // 256, ids % 256]).astype(BF16)
    digits = in_order(
        lax.ppermute(digits, ALL, swap_route(0)), lax.ppermute(digits, ALL, swap_route(1)), 0
    )
    first, second = grad_out.T[:cw], grad_out.T[cw:]
    cot = in_order(
        lax.ppermute(jnp.where(odd, second, first), ALL, turn(0)),
        lax.ppermute(jnp.where(odd, first, second), ALL, turn(1)),
        0,
    )
    cot = jnp.concatenate([cot, jnp.pad(digits, ((0, 12), (0, 0)))], axis=0)
    cot, weights = lax.optimization_barrier((cot, weights))
    own = gather(cot, "chip", nc)
    other = flip(own)

    def ids_of(cot):
        digits = cot[:, fw : fw + 4].astype(jnp.int32)
        all_ids = 256 * digits[:, 0::2] + digits[:, 1::2]
        return (all_ids - v * entries).reshape(nc, 1, 2 * toks)

    own_ids, other_ids = ids_of(own), ids_of(other)

    shares = grad_products(place, weights, own, other, nb)
    shares = lax.all_to_all(shares, "yhi", 0, 0, tiled=True)
    pieces = lookup(own_ids, table) + flip(lookup(other_ids, table))
    pieces, shares = lax.optimization_barrier((pieces, shares))
    grads = jnp.sum(shares.astype(F32), axis=0)
    pieces = lax.all_to_all(pieces, "chip", 0, 0, tiled=True)
    cols = jnp.sum(pieces.astype(F32), axis=0).astype(BF16)
    embed = jnp.concatenate([cols[:, :toks], cols[:, toks:]], axis=0)
    embed = lax.ppermute(embed, ALL, across).astype(F32)

    def by_block(x):
        return jnp.sum(x.reshape(2, cw, toks), axis=1)

    def to_rows(x):
        return jnp.broadcast_to(x[:, None], (2, cw, toks)).reshape(2 * cw, toks)

    hid = hidden.T.astype(F32)
    gain_e = jnp.where(odd, gain_embed[cw:], gain_embed[:cw])
    gain_e, gain_h = jnp.concatenate([gain_e, gain_e])[:, None], gain_hidden[:, None]
    grad_left, grad_right = grads[:fw], grads[fw:]
    dn_embed, dn_hidden = grad_left * gain_e, grad_right * gain_h
    halves = jnp.concatenate([by_block(embed * embed), by_block(dn_embed * embed)], axis=0)
    halves += lax.ppermute(halves, "yhi", [(i, i ^ 1) for i in range(nb)])
    stats = jnp.concatenate(
        [
            halves,
            jnp.sum(hid * hid, axis=0, keepdims=True),
            jnp.sum(dn_hidden * hid, axis=0, keepdims=True),
        ],
        axis=0,
    )
    stats = jnp.sum(gather(stats, VOCAB, nv), axis=0)
    inv_embed = lax.rsqrt(stats[:2] / full + EPS)
    coef_embed = to_rows(stats[2:4] * inv_embed / full)
    inv_embed = to_rows(inv_embed)
    inv_hidden = lax.rsqrt(stats[4:5] / full + EPS)
    coef_hidden = stats[5:6] * inv_hidden / full
    norm_embed, norm_hidden = embed * inv_embed, hid * inv_hidden
    grad_embedded = (inv_embed * (dn_embed - norm_embed * coef_embed)).astype(BF16)
    grad_hidden = (inv_hidden * (dn_hidden - norm_hidden * coef_hidden)).astype(BF16)

    gains = jnp.sum(grad_left * norm_embed, axis=1)
    gains = gains[:cw] + gains[cw:]
    gains = jnp.concatenate(
        [
            jnp.where(odd, 0.0, gains),
            jnp.where(odd, gains, 0.0),
            jnp.sum(grad_right * norm_hidden, axis=1),
        ]
    )
    lines = -(-2 * fw // toks)
    gains = jnp.pad(gains, (0, lines * toks - 2 * fw)).reshape(lines, toks)
    gains = jnp.pad(gains, ((0, 16 - lines), (0, 0)))
    gains_high = gains.astype(BF16)
    gains_low = (gains - gains_high.astype(F32)).astype(BF16)
    normed = gather(
        jnp.concatenate(
            [
                (norm_embed * gain_e).astype(BF16),
                (norm_hidden * gain_h).astype(BF16),
                gains_high,
                gains_low,
            ],
            axis=0,
        ),
        "yhi",
        nb,
    )

    mine = lax.ppermute(grad_embedded, ALL, across)

    normed, mine = lax.optimization_barrier((normed, mine))
    keep, send, weight_terms = out_products(place, weights, own, other, normed)
    terms = (keep.astype(F32) + flip(send).astype(F32)).astype(BF16)
    mine = jnp.broadcast_to(mine[None], (nc,) + mine.shape)
    both = lax.all_to_all(
        jnp.concatenate([terms, mine], axis=1), "chip", 0, 0, tiled=True
    )
    own_rows = both[:, fw:]
    grad_table, done = scatter(
        jnp.concatenate([own_ids, other_ids], axis=0), own_rows, flip(own_rows), entries
    )

    terms = jnp.sum(both[:, :fw].astype(F32), axis=0).astype(BF16)
    first, second = terms[:cw], terms[cw:]
    got0 = lax.ppermute(jnp.where(odd, second, first), ALL, turn_back(0))
    got1 = lax.ppermute(jnp.where(odd, first, second), ALL, turn_back(1))
    weight_terms = lax.psum_scatter(
        weight_terms.reshape(na * (cw + PAD_ROWS), 2 * fw), "z", scatter_dimension=0, tiled=True
    )
    projected, grad_embed, grad_hid, grad_gains = finish(
        place, weight_terms, got0, got1, done, lines
    )
    return (projected.T, grad_hidden.T, grad_table, grad_embed, grad_hid, grad_gains)


def solution(mesh):
    nv, nd = mesh.shape["vocab"], mesh.shape["dp"]
    nb = min(4, nd)
    split = Mesh(mesh.devices.reshape(nv // 2, 2, nd // nb, nb), ALL)
    rows = P(DP, VOCAB)
    return jax.shard_map(
        per_device,
        mesh=split,
        in_specs=(
            P(DP),
            rows,
            rows,
            P(VOCAB),
            P(VOCAB),
            P(VOCAB, DP),
            P(VOCAB, DP),
            rows,
        ),
        out_specs=(rows, rows, rows, P(VOCAB, DP), P(VOCAB, DP), P(None, VOCAB)),
        check_vma=False,
    )
```
